32 devices in a mesh: ep: 8 (over y, x, core), ex: 4 (over z).
Axes of the slice: x: 2, y: 2, z: 4, core: 2. Of those that a mesh axis runs over, the one named last changes fastest.
Arguments:
- dout: bfloat16 [1024, 7168], P(('ep', 'ex')), may hold values from -1.5 to 1.5
- gates: bfloat16 [1024, 8], P(('ep', 'ex')), may hold values from 0.049804688 to 0.59765625
- saved_down_input: bfloat16 [1024, 8, 1024], P(('ep', 'ex')), may hold values from -3 to 3
- routing: int32 [1024, 8], P(('ep', 'ex')), may hold values from 0 to 27, as said below
- placement: int32 [32], replicated, may hold values from 0 to 27, as said below
- partner: int32 [32], replicated, may hold values from 0 to 31, as said below
- frozen: bfloat16 [32, 1024, 7168], P(('ep', 'ex')), as said below
- colscale: float32 [32, 7168], P(('ep', 'ex')), may hold values from 0.5 to 2, as said below
- adapter_down_factor: bfloat16 [32, 1024, 64], P(('ep', 'ex')), as said below
- adapter_up_factor: bfloat16 [32, 64, 7168], P(('ep', 'ex')), as said below
- first_moment_down: bfloat16 [32, 1024, 64], P(('ep', 'ex')), as said below
- second_moment_down: bfloat16 [32, 1024, 64], P(('ep', 'ex')), may hold values from 0.1 to 4, as said below
- first_moment_up: bfloat16 [32, 64, 7168], P(('ep', 'ex')), as said below
- second_moment_up: bfloat16 [32, 64, 7168], P(('ep', 'ex')), may hold values from 0.1 to 4, as said below
Outputs:
- routed_input_gradient: bfloat16 [1024, 8, 1024], P(('ep', 'ex'))
- combine_gate_gradient: bfloat16 [1024, 8], P(('ep', 'ex'))
- updated_down_factor: bfloat16 [32, 1024, 64], P(('ep', 'ex'))
- updated_up_factor: bfloat16 [32, 64, 7168], P(('ep', 'ex'))
- updated_first_moment_down: bfloat16 [32, 1024, 64], P(('ep', 'ex'))
- updated_second_moment_down: bfloat16 [32, 1024, 64], P(('ep', 'ex'))
- updated_first_moment_up: bfloat16 [32, 64, 7168], P(('ep', 'ex'))
- updated_second_moment_up: bfloat16 [32, 64, 7168], P(('ep', 'ex'))
The draws below stay inside these ranges and needn't reach their ends.
Inputs may be any that keep to these rules, and one draw needn't show every extreme that they name: `routing`: each token names 8 different experts. Of each device's tokens, an expert with two slots is named by exactly 16, every other expert by exactly 8. `placement`: every expert is held by one slot, or by two slots of one expert group (equal index along ep); 4 experts hold two slots, each in a group of its own. placement[partner[s]] = placement[s]; partner[s] is the other slot of the same expert, or s if the expert holds one slot. `frozen`: slots of the same expert hold equal values. `colscale`: slots of the same expert hold equal values. `adapter_down_factor`: slots of the same expert hold equal values. `adapter_up_factor`: slots of the same expert hold equal values. `first_moment_down`: slots of the same expert hold equal values. `second_moment_down`: slots of the same expert hold equal values. `first_moment_up`: slots of the same expert hold equal values. `second_moment_up`: slots of the same expert hold equal values.
All inputs are finite; a program needn't handle non-finite values.
Results may differ from the reference program's by a relative error of at most 0.005.
Values may be sent and summed in bfloat16 or wider, within the bound.
No kernel may reach another device: no remote copies, remote signals or barrier semaphores. Data moves between devices by JAX's collectives and lax.ppermute only.
A program may use at most 128 MiB of HBM per device.

```python
import math
import jax
import jax.numpy as jnp
from jax import lax

D = 7168
TOP = 8
H = 1024
R = 64
TOK_DEV = 32
GROUP = 4
SLOTS = 32
HOT = 4
EXPERTS = 28
CAP = 8
TOKENS = 1024


def layout(key):
    group_count = SLOTS // GROUP
    hot_key = jax.random.fold_in(key, 7001)
    pair_key = jax.random.fold_in(key, 7002)
    perm_key = jax.random.fold_in(key, 7003)
    group_order = jax.random.permutation(hot_key, group_count)
    hot_group = jnp.zeros((group_count,), jnp.int32).at[group_order[:HOT]].set(1)
    pair_keys = jax.random.split(pair_key, group_count)
    members = jax.vmap(lambda one_key: jax.random.permutation(one_key, GROUP)[:2])(pair_keys).astype(jnp.int32)
    low_member = jnp.min(members, axis=1)
    high_member = jnp.max(members, axis=1)
    slot_ids = jnp.arange(SLOTS, dtype=jnp.int32)
    group_of = slot_ids // GROUP
    within = slot_ids % GROUP
    hot_slot = hot_group[group_of] == 1
    low_slot = low_member[group_of]
    high_slot = high_member[group_of]
    partner = jnp.where(hot_slot & (within == low_slot), group_of * GROUP + high_slot, jnp.where(hot_slot & (within == high_slot), group_of * GROUP + low_slot, slot_ids)).astype(jnp.int32)
    second = (hot_slot & (within == high_slot)).astype(jnp.int32)
    rank_ids = (jnp.cumsum(1 - second) - 1).astype(jnp.int32)
    expert_perm = jax.random.permutation(perm_key, EXPERTS).astype(jnp.int32)
    first_pick = expert_perm[rank_ids]
    placement = jnp.where(second == 1, first_pick[partner], first_pick).astype(jnp.int32)
    return (placement, partner, second)


def draw_placement(key, part):
    return layout(key)[0]


def draw_partner(key, part):
    return layout(key)[1]


def draw_routing(key, part):
    placement, partner, second = layout(key)
    hot_flag = jnp.zeros((EXPERTS,), jnp.int32).at[placement].max(second)
    hot_ids = jnp.argsort(1 - hot_flag, stable=True)[:HOT].astype(jnp.int32)
    cold_ids = jnp.argsort(hot_flag, stable=True)[:EXPERTS - HOT].astype(jnp.int32)
    labels = jnp.sort(jnp.concatenate([jnp.repeat(hot_ids, 2 * CAP), jnp.repeat(cold_ids, CAP)]))

    def one_device(device_key):
        token_key = jax.random.fold_in(device_key, 3)
        turn_key = jax.random.fold_in(device_key, 4)
        token_grid = labels.reshape(TOP, TOK_DEV).T
        token_grid = token_grid[jax.random.permutation(token_key, TOK_DEV)]
        rotation = jax.random.randint(turn_key, (TOK_DEV, 1), 0, TOP)
        column_ids = (jnp.arange(TOP, dtype=jnp.int32)[None, :] + rotation) % TOP
        return jnp.take_along_axis(token_grid, column_ids, axis=1)
    device_keys = jax.random.split(jax.random.fold_in(key, 7100), SLOTS)
    return jax.vmap(one_device)(device_keys).reshape(TOKENS, TOP).astype(jnp.int32)


def per_slot(key, tag, sampler):
    placement, partner, second = layout(key)
    source = jnp.minimum(jnp.arange(SLOTS, dtype=jnp.int32), partner)
    base_key = jax.random.fold_in(key, tag)
    return lax.map(lambda one_slot: sampler(jax.random.fold_in(base_key, one_slot)), source)


def draw_frozen(key, part):
    return per_slot(key, 8001, lambda slot_key: (jax.random.normal(slot_key, (H, D), jnp.float32) * H ** (-0.5)).astype(jnp.bfloat16))


def draw_colscale(key, part):
    return per_slot(key, 8002, lambda slot_key: jnp.exp(jax.random.uniform(slot_key, (D,), jnp.float32, jnp.log(0.5), jnp.log(2.0))))


def draw_adapter_down_factor(key, part):
    return per_slot(key, 8003, lambda slot_key: (jax.random.normal(slot_key, (H, R), jnp.float32) * H ** (-0.5)).astype(jnp.bfloat16))


def draw_adapter_up_factor(key, part):
    return per_slot(key, 8004, lambda slot_key: (jax.random.normal(slot_key, (R, D), jnp.float32) * 0.02).astype(jnp.bfloat16))


def draw_first_moment_down(key, part):
    return per_slot(key, 8005, lambda slot_key: jax.random.normal(slot_key, (H, R), jnp.float32).astype(jnp.bfloat16))


def draw_second_moment_down(key, part):
    return per_slot(key, 8006, lambda slot_key: jnp.exp(jax.random.uniform(slot_key, (H, R), jnp.float32, jnp.log(0.1), jnp.log(4.0))).astype(jnp.bfloat16))


def draw_first_moment_up(key, part):
    return per_slot(key, 8007, lambda slot_key: jax.random.normal(slot_key, (R, D), jnp.float32).astype(jnp.bfloat16))


def draw_second_moment_up(key, part):
    return per_slot(key, 8008, lambda slot_key: jnp.exp(jax.random.uniform(slot_key, (R, D), jnp.float32, jnp.log(0.1), jnp.log(4.0))).astype(jnp.bfloat16))


def shard_levels(key, extent, shards, low, largest):
    factor_of, own = 1.0, jax.random.fold_in(key, 6)
    for position, blocks in shards:
        steps = jnp.exp(jax.random.uniform(jax.random.fold_in(own, position), (blocks,), jnp.float32, low / len(shards), largest / len(shards)))
        factor_of = factor_of * jnp.repeat(steps, extent[position] // blocks).reshape([-1 if axis == position else 1 for axis in range(len(extent))])
    return factor_of


def scatter_about(rng, shape, width, reach, cuts=(), held_as=jnp.bfloat16):
    drawn = jax.random.normal(rng, shape, jnp.float32) * width
    if len(cuts) > 0:
        drawn = shard_levels(rng, shape, cuts, -0.22, 0.18) * drawn
    return jnp.clip(drawn, min=-reach, max=reach).astype(held_as)


def setup_inputs(seed: int = 0) -> dict:
    splits = jax.random.split(jax.random.key(seed), 15)
    return {
        "dout": scatter_about(splits[0], (TOKENS, D), 0.25, 1.5, ((0, 32),)),
        "gates": jnp.clip(jnp.exp(math.log(0.59765625) - 2.4849066 * jax.random.uniform(splits[1], (TOKENS, TOP), jnp.float32) ** shard_levels(splits[1], (TOKENS, TOP), ((0, 32),), -0.2, 0.2)), 0.049804688, 0.59765625).astype(jnp.bfloat16),
        "saved_down_input": scatter_about(splits[2], (TOKENS, TOP, H), 0.5, 3.0, ((0, 32),)),
        "routing": draw_routing(jax.random.fold_in(splits[14], 71), 0),
        "placement": draw_placement(jax.random.fold_in(splits[14], 71), 0),
        "partner": draw_partner(jax.random.fold_in(splits[14], 71), 0),
        "frozen": draw_frozen(jax.random.fold_in(splits[14], 71), 0),
        "colscale": draw_colscale(jax.random.fold_in(splits[14], 71), 0),
        "adapter_down_factor": draw_adapter_down_factor(jax.random.fold_in(splits[14], 71), 0),
        "adapter_up_factor": draw_adapter_up_factor(jax.random.fold_in(splits[14], 71), 0),
        "first_moment_down": draw_first_moment_down(jax.random.fold_in(splits[14], 71), 0),
        "second_moment_down": draw_second_moment_down(jax.random.fold_in(splits[14], 71), 0),
        "first_moment_up": draw_first_moment_up(jax.random.fold_in(splits[14], 71), 0),
        "second_moment_up": draw_second_moment_up(jax.random.fold_in(splits[14], 71), 0),
    }


adapter_scale = 2.0
beta_one = 0.9
beta_two = 0.999
adam_eps = 1e-08
learn_rate = 0.01
weight_decay = 0.01
adam_step = 10

def expert_row_block(hidden_row_block, output_gradient_rows, gate_row_values, frozen_w, scale, adapter_down_projected, low_b):
    gate_broadcast_wide = gate_row_values.astype(jnp.float32)[:, None]
    dout_wide = output_gradient_rows.astype(jnp.float32)
    adapter_output_gradient = (gate_broadcast_wide * dout_wide).astype(jnp.bfloat16)
    dsc_low = (dout_wide * scale[None, :]).astype(jnp.bfloat16)
    backward_through_adapter = jnp.dot(adapter_output_gradient, low_b.T, preferred_element_type=jnp.float32).astype(jnp.bfloat16)
    backward_through_frozen = jnp.dot(dsc_low, frozen_w.T, preferred_element_type=jnp.float32)
    incoming_input_gradient = gate_broadcast_wide * backward_through_frozen + adapter_scale * jnp.dot(backward_through_adapter, adapter_down_projected.T, preferred_element_type=jnp.float32)
    adapter_down_product = jnp.dot(hidden_row_block, adapter_down_projected, preferred_element_type=jnp.float32).astype(jnp.bfloat16)
    output_gradient_adapter = jnp.dot(output_gradient_rows, low_b.T, preferred_element_type=jnp.float32)
    gated_output = lax.optimization_barrier(jnp.sum(hidden_row_block.astype(jnp.float32) * backward_through_frozen, axis=1)) + adapter_scale * lax.optimization_barrier(jnp.sum(adapter_down_product.astype(jnp.float32) * output_gradient_adapter, axis=1))
    down_factor_gradient = adapter_scale * jnp.dot(hidden_row_block.T, backward_through_adapter, preferred_element_type=jnp.float32)
    up_factor_gradient = adapter_scale * jnp.dot(adapter_down_product.T, adapter_output_gradient, preferred_element_type=jnp.float32)
    return (incoming_input_gradient.astype(jnp.bfloat16), gated_output.astype(jnp.bfloat16), down_factor_gradient, up_factor_gradient)

def apply_adam_update(weights, moment, second_moment, gradient):
    weights_wide = weights.astype(jnp.float32)
    first = beta_one * moment.astype(jnp.float32) + (1.0 - beta_one) * gradient
    second = beta_two * second_moment.astype(jnp.float32) + (1.0 - beta_two) * gradient * gradient
    first_hat = first / (1.0 - beta_one ** adam_step)
    second_hat = second / (1.0 - beta_two ** adam_step)
    fresh = weights_wide - learn_rate * (first_hat / (jnp.sqrt(second_hat) + adam_eps) + weight_decay * weights_wide)
    return (fresh.astype(jnp.bfloat16), first.astype(jnp.bfloat16), second.astype(jnp.bfloat16))

def slot_gradient(expert_gradients, placement, partner):
    mate_expert = placement[partner]
    differs = (mate_expert != placement).astype(jnp.float32)[:, None, None]
    return expert_gradients[placement] + differs * expert_gradients[mate_expert]

def reference(dout, gates, saved_down_input, routing, placement, partner, frozen, colscale, adapter_down_factor, adapter_up_factor, first_moment_down, second_moment_down, first_moment_up, second_moment_up):
    row_count = TOKENS * TOP
    expert_flat = routing.reshape(row_count).astype(jnp.int32)
    hidden_flat = saved_down_input.reshape(row_count, H)
    gate_flat = gates.reshape(row_count)
    expert_ids = jnp.arange(EXPERTS, dtype=jnp.int32)
    counts = lax.optimization_barrier(jnp.sum((expert_flat[:, None] == expert_ids[None, :]).astype(jnp.int32), axis=0)).astype(jnp.int32)
    row_order = jnp.argsort(expert_flat, stable=True).astype(jnp.int32)
    starts = (jnp.cumsum(counts) - counts).astype(jnp.int32)
    slot_ids = jnp.arange(SLOTS, dtype=jnp.int32)
    home_slot = lax.optimization_barrier(jnp.min(jnp.where(placement[None, :] == expert_ids[:, None], slot_ids[None, :], SLOTS), axis=1)).astype(jnp.int32)
    by_load = jnp.argsort(-counts, stable=True).astype(jnp.int32)
    padded_order = jnp.concatenate([row_order, jnp.zeros((2 * CAP * SLOTS,), jnp.int32)])
    zero_low = jnp.zeros((), jnp.bfloat16)

    def run(expert, room_rows):
        row_pick = lax.dynamic_slice(padded_order, (starts[expert].astype(jnp.int32),), (room_rows,))
        is_live = jnp.arange(room_rows, dtype=jnp.int32) < counts[expert]
        current_slot = home_slot[expert]
        hidden_row_block = jnp.where(is_live[:, None], hidden_flat[row_pick], zero_low)
        output_gradient_rows = jnp.where(is_live[:, None], dout[row_pick // TOP], zero_low)
        gate_row_values = jnp.where(is_live, gate_flat[row_pick], zero_low)
        backward_outputs = expert_row_block(hidden_row_block, output_gradient_rows, gate_row_values, frozen[current_slot], colscale[current_slot], adapter_down_factor[current_slot], adapter_up_factor[current_slot])
        return backward_outputs + (jnp.where(is_live, row_pick, row_count).astype(jnp.int32),)
    hot_out = lax.map(lambda expert: run(expert, 2 * CAP * SLOTS), by_load[:HOT])
    cold_out = lax.map(lambda expert: run(expert, CAP * SLOTS), by_load[HOT:])
    row_places = jnp.concatenate([hot_out[4].reshape(-1), cold_out[4].reshape(-1)])
    grad_rows = jnp.concatenate([hot_out[0].reshape(-1, H), cold_out[0].reshape(-1, H)])
    gate_rows_out = jnp.concatenate([hot_out[1].reshape(-1), cold_out[1].reshape(-1)])
    routed_input_gradient = jnp.zeros((row_count, H), jnp.bfloat16).at[row_places].set(grad_rows, mode='drop').reshape(TOKENS, TOP, H)
    combine_gate_gradient = jnp.zeros((row_count,), jnp.bfloat16).at[row_places].set(gate_rows_out, mode='drop').reshape(TOKENS, TOP)
    down_factor_gradients = jnp.zeros((EXPERTS, H, R), jnp.float32).at[by_load].set(jnp.concatenate([hot_out[2], cold_out[2]]))
    up_factor_gradients = jnp.zeros((EXPERTS, R, D), jnp.float32).at[by_load].set(jnp.concatenate([hot_out[3], cold_out[3]]))
    updated_down_factor, updated_first_moment_down, updated_second_moment_down = apply_adam_update(adapter_down_factor, first_moment_down, second_moment_down, slot_gradient(down_factor_gradients, placement, partner))
    updated_up_factor, updated_first_moment_up, updated_second_moment_up = apply_adam_update(adapter_up_factor, first_moment_up, second_moment_up, slot_gradient(up_factor_gradients, placement, partner))
    return (routed_input_gradient, combine_gate_gradient, updated_down_factor, updated_up_factor, updated_first_moment_down, updated_second_moment_down, updated_first_moment_up, updated_second_moment_up)
```

```python
import functools

import jax
import jax.numpy as jnp
from jax import lax
from jax.experimental import pallas as pl
from jax.experimental.pallas import tpu as pltpu
from jax.sharding import PartitionSpec as P

adapter_scale = 2.0
beta_one = 0.9
beta_two = 0.999
adam_eps = 1e-08
learn_rate = 0.01
weight_decay = 0.01
adam_step = 10

TILE = 512
LANES = 128
SHARES = (5, 6, 3)
VMEM_LIMIT = 24 * 1024 * 1024
EXPERT_VMEM_LIMIT = 44 * 1024 * 1024
bf16 = jnp.bfloat16
f32 = jnp.float32


def chunk_widths(width):
    tiles = width // TILE
    total = sum(SHARES)
    edges = [0]
    taken = 0
    for share in SHARES:
        taken += share
        edges.append(tiles * taken // total)
    return [(edges[i] * TILE, (edges[i + 1] - edges[i]) * TILE) for i in range(len(SHARES)) if edges[i + 1] > edges[i]]


def log2(n):
    k = n.bit_length() - 1
    assert 1 << k == n
    return k


def iota(shape, dim):
    return lax.broadcasted_iota(jnp.int32, shape, dim)


def dot(a, b, ca, cb):
    return lax.dot_general(a, b, (((ca,), (cb,)), ((), ())), preferred_element_type=f32)


HBM = pl.BlockSpec(memory_space=pltpu.HBM)
VMEM = pl.BlockSpec(memory_space=pltpu.VMEM)
SMEM = pl.BlockSpec(memory_space=pltpu.SMEM)
ANY = pl.BlockSpec(memory_space=pl.ANY)
DMA = pltpu.SemaphoreType.DMA


def fetch(pairs, sems):
    copies = [pltpu.make_async_copy(src, dst, sems.at[i]) for i, (src, dst) in enumerate(pairs)]
    for copy in copies:
        copy.start()
    return copies


def call(kernel, outs, flops=0, moved=0, limit=VMEM_LIMIT, **kw):
    params = pltpu.CompilerParams(vmem_limit_bytes=limit)
    cost = pl.CostEstimate(flops=flops, bytes_accessed=moved, transcendentals=0)
    return pl.pallas_call(kernel, out_shape=outs, compiler_params=params, cost_estimate=cost, **kw)


def index_kernel(dims, width, rout_hbm, place_hbm, dout_hbm, hot_ref, chunk_ref, rest_ref, rout_ref, place_ref, sems):
    rest_width = rest_ref.shape[1]
    copies = fetch(
        [
            (rout_hbm, rout_ref),
            (place_hbm, place_ref),
            (dout_hbm.at[:, pl.ds(0, width)], chunk_ref.at[:, pl.ds(0, width)]),
            (dout_hbm.at[:, pl.ds(width, rest_width)], rest_ref),
        ],
        sems,
    )
    copies[0].wait()
    copies[1].wait()
    tok, top, rows, slots, groups, members, cap = dims
    kt = log2(top)
    rid_c, rid_r = iota((rows, 1), 0), iota((1, rows), 1)
    spread = (lax.shift_right_logical(iota((rows, tok), 0), kt) == iota((rows, tok), 1)).astype(bf16)
    routes = rout_ref[...].astype(f32).astype(bf16)
    wide = dot(spread, routes, 1, 1)
    e_col = jnp.sum(jnp.where((iota((rows, top), 0) & (top - 1)) == iota((rows, top), 1), wide, 0.0), axis=1, keepdims=True)
    tall = dot(routes, spread, 1, 1)
    e_row = jnp.sum(jnp.where((iota((top, rows), 1) & (top - 1)) == iota((top, rows), 0), tall, 0.0), axis=0, keepdims=True)
    earlier = rid_r < rid_c
    turn = jnp.sum(jnp.where((e_col == e_row) & earlier, 1.0, 0.0), axis=1, keepdims=True).astype(jnp.int32)
    holds = e_col == place_ref[...].astype(f32)
    slot = iota((rows, slots), 1).astype(f32)
    first = jnp.min(jnp.where(holds, slot, float(slots)), axis=1, keepdims=True)
    last = jnp.max(jnp.where(holds, slot, -1.0), axis=1, keepdims=True)
    target = jnp.where((turn & 1) == 1, last, first)
    target_row = jnp.sum(jnp.where(rid_c == rid_r, target, 0.0), axis=0, keepdims=True)
    pos = jnp.sum(jnp.where((target == target_row) & earlier, 1.0, 0.0), axis=1, keepdims=True).astype(jnp.int32)
    target = target.astype(jnp.int32)
    place = target * cap + pos
    place_z = ((target & (members - 1)) * groups + lax.shift_right_logical(target, log2(members))) * cap + pos
    hot_ref[...] = (place == rid_r).astype(f32).astype(bf16)
    hot_z = (place_z == rid_r).astype(f32).astype(bf16)
    chunk_ref[:, width:] = dot(spread, hot_z, 0, 0).astype(bf16)
    copies[2].wait()
    copies[3].wait()


def tied_kernel(*refs):
    pass


def tied(x, *after):
    return call(
        tied_kernel,
        shape(x.shape),
        in_specs=[ANY] * (1 + len(after)),
        out_specs=ANY,
        input_output_aliases={0: 0},
    )(x, *after)


def hidden_kernel(dims, hot_ref, gate_hbm, hidden_hbm, after_ref, out_ref, gate_ref, hidden_ref, sems):
    tok, top, rows = dims[:3]
    copies = fetch([(gate_hbm, gate_ref), (hidden_hbm, hidden_ref)], sems)
    copies[0].wait()
    width = hidden_ref.shape[1]
    hot = hot_ref[...]
    spread = (lax.shift_right_logical(iota((rows, tok), 0), log2(top)) == iota((rows, tok), 1)).astype(bf16)
    wide = dot(spread, gate_ref[...], 1, 1)
    gate = jnp.sum(jnp.where((iota((rows, top), 0) & (top - 1)) == iota((rows, top), 1), wide, 0.0), axis=1, keepdims=True)
    out_ref[:, width:] = dot(hot, jnp.broadcast_to(gate, (rows, LANES)).astype(bf16), 0, 0).astype(bf16)
    copies[1].wait()
    out_ref[:, :width] = dot(hot, hidden_ref[...], 0, 0).astype(bf16)


def place_direct_kernel(members, *refs):
    out_ref = refs[-1]
    me = lax.axis_index("ex")
    tok = refs[0].shape[0]
    for s in range(members):
        out_ref[pl.ds(pl.multiple_of((me ^ s) * tok, tok), tok), :] = refs[s][...]


def place_relay_kernel(own, near, far, far_near, end, end_near, *refs):
    out_ref = refs[-1]
    me = lax.axis_index("ex")
    tok = own.shape[0]
    orders = (
        (own, near, end, end_near),
        (near, own, far, far_near),
        (far_near, far, own, near),
        (end_near, end, near, own),
    )
    for z, order in enumerate(orders):

        @pl.when(me == z)
        def _():
            for i, ref in enumerate(order):
                out_ref[i * tok : (i + 1) * tok, :] = ref[...]


def pick_kernel(dims, own_ref, other_ref, pick_ref):
    tok, top, rows, slots, groups, members, cap = dims
    tokens = members * tok
    ep, z = lax.axis_index("ep"), lax.axis_index("ex")
    chip, core = lax.shift_right_logical(ep, 1), ep & 1
    row, q = iota((rows, rows), 0), iota((rows, rows), 1)
    p = row & (cap - 1)
    step = lax.shift_right_logical(row, log2(2 * members * cap))
    wanted = (z * groups + (step ^ chip) * 2 + core) * cap + p
    choose = (wanted == q).astype(f32).astype(bf16)
    for b, ref in enumerate((own_ref, other_ref)):
        found = dot(choose, ref[...], 1, 1)
        r = iota((rows, tokens), 0)
        from_core = lax.shift_right_logical(r, log2(members * cap)) & 1
        from_z = lax.shift_right_logical(r, log2(cap)) & (members - 1)
        t = lax.shift_right_logical(iota((rows, tokens), 1), log2(tok))
        keep = (from_core == (core ^ b)) & (from_z == t)
        pick_ref[:, b * tokens : (b + 1) * tokens] = jnp.where(keep, found, 0.0).astype(bf16)


def rows_kernel(start, width, steps, pick_ref, own_ref, other_ref, *out_refs):
    out_refs = out_refs[-steps:]
    tokens = own_ref.shape[0]
    block = out_refs[0].shape[0]
    pick = pick_ref[...]
    for j in range(width // TILE):
        cols = slice(j * TILE, (j + 1) * TILE)
        took = slice(start + j * TILE, start + (j + 1) * TILE)
        got = dot(pick[:, :tokens], own_ref[:, took], 1, 0) + dot(pick[:, tokens:], other_ref[:, took], 1, 0)
        for s, ref in enumerate(out_refs):
            ref[:, cols] = got[s * block : (s + 1) * block].astype(bf16)


def order_by_step(ref, steps, block, cols):
    chip = lax.shift_right_logical(lax.axis_index("ep"), 1)
    return jnp.concatenate(
        [ref[pl.ds(pl.multiple_of((chip ^ s) * block, block), block), cols] for s in range(steps)], axis=0
    )


def low_kernel(steps, block, arrived_ref, down_ref, low_ref, gated_ref):
    hidden = down_ref.shape[1]
    rows = order_by_step(arrived_ref, steps, block, slice(0, hidden))
    gate = order_by_step(arrived_ref, steps, block, slice(hidden, hidden + LANES))[:, :1].astype(f32)
    low = dot(rows, down_ref[...], 1, 1).astype(bf16)
    low_ref[...] = low
    gated_ref[...] = (adapter_scale * gate * low.astype(f32)).astype(bf16)


def up_grad_kernel(steps, *refs):
    blocks, gated_ref, out_ref = refs[:steps], refs[steps], refs[-1]
    for j in range(out_ref.shape[1] // TILE):
        cols = slice(j * TILE, (j + 1) * TILE)
        rows = jnp.concatenate([b[:, cols] for b in blocks], axis=0)
        out_ref[:, cols] = dot(gated_ref[...], rows, 0, 0).astype(bf16)


def expert_kernel(steps, off, unread, first, final, *refs):
    blocks = refs[:steps]
    width = blocks[0].shape[1]
    tiles = width // TILE
    refs = refs[steps:]
    frozen_hbm, scale_hbm, up_hbm = refs[:3]
    refs = refs[3 + unread :]
    frozen_ref, scale_ref, up_ref, sems = refs[-4:]
    refs = refs[:-4]
    copies = fetch(
        [(scale_hbm.at[:, pl.ds(off, width)], scale_ref)]
        + [(frozen_hbm.at[:, pl.ds(off + j * TILE, TILE)], frozen_ref.at[j]) for j in range(tiles)]
        + [(up_hbm.at[:, pl.ds(off, width)], up_ref)],
        sems,
    )
    if not first:
        back_in, low_in = refs[:2]
        refs = refs[2:]
    if final:
        gated_ref, arrived_ref, down_ref, low_ref = refs[:4]
        up_grad_ref, ret_ref, back_ref, thin_ref = refs[4:]
        for j in range(tiles):
            cols = slice(j * TILE, (j + 1) * TILE)
            rows = jnp.concatenate([b[:, cols] for b in blocks], axis=0)
            up_grad_ref[:, cols] = dot(gated_ref[...], rows, 0, 0).astype(bf16)
    else:
        back_ref, thin_ref = refs
    copies[0].wait()
    for j in range(tiles):
        cols = slice(j * TILE, (j + 1) * TILE)
        rows = jnp.concatenate([b[:, cols] for b in blocks], axis=0)
        scaled = (rows.astype(f32) * scale_ref[:, cols]).astype(bf16)
        copies[1 + j].wait()
        part = dot(scaled, frozen_ref[j], 1, 1)
        if j > 0:
            part += back_ref[...]
        elif not first:
            part += back_in[...]
        back_ref[...] = part
    copies[1 + tiles].wait()
    thin = dot(jnp.concatenate([b[...] for b in blocks], axis=0), up_ref[...], 1, 1)
    thin_ref[...] = thin if first else thin + low_in[...]
    if final:
        block = blocks[0].shape[0]
        hidden = down_ref.shape[1]
        chip = lax.shift_right_logical(lax.axis_index("ep"), 1)
        saved = order_by_step(arrived_ref, steps, block, slice(0, hidden))
        gate = order_by_step(arrived_ref, steps, block, slice(hidden, hidden + LANES))[:, :1].astype(f32)
        back = back_ref[...]
        thin = thin_ref[...]
        back_low = (gate * thin).astype(bf16)
        grad = (gate * back + adapter_scale * dot(back_low, down_ref[...], 1, 0)).astype(bf16)
        gate_grad = jnp.sum(saved.astype(f32) * back, axis=1, keepdims=True) + adapter_scale * jnp.sum(
            low_ref[...].astype(f32) * thin, axis=1, keepdims=True
        )
        gate_grad = jnp.broadcast_to(gate_grad, (gate_grad.shape[0], LANES)).astype(bf16)
        for s in range(steps):
            at = pl.ds(pl.multiple_of((chip ^ s) * block, block), block)
            ret_ref[at, :hidden] = grad[s * block : (s + 1) * block]
            ret_ref[at, hidden:] = gate_grad[s * block : (s + 1) * block]
        up_grad_ref[:, width:] = (adapter_scale * dot(back_low, saved, 0, 0)).astype(bf16)


def adam_math(weights, moment, second_moment, gradient):
    weights_wide = weights.astype(f32)
    first = beta_one * moment.astype(f32) + (1.0 - beta_one) * gradient
    second = beta_two * second_moment.astype(f32) + (1.0 - beta_two) * gradient * gradient
    first_hat = first * (1.0 / (1.0 - beta_one**adam_step))
    second_hat = second * (1.0 / (1.0 - beta_two**adam_step))
    fresh = weights_wide - learn_rate * (
        first_hat / (jnp.sqrt(second_hat) + adam_eps) + weight_decay * weights_wide
    )
    return (fresh.astype(bf16), first.astype(bf16), second.astype(bf16))


def pair(partner_ref, members):
    z = lax.axis_index("ex")
    return z, partner_ref[lax.axis_index("ep") * members + z] & (members - 1)


def onward_kernel(members, hop, partner_ref, own_ref, got_ref, *refs):
    out_ref = refs[-1]
    z, mate = pair(partner_ref, members)
    if hop == 2:
        mine = ((z == 1) & (mate >= 2)) | ((z == 2) & (mate <= 1))
    else:
        mine = ((z == 1) & (mate == 0)) | ((z == 2) & (mate == 3))

    @pl.when(mine)
    def _():
        out_ref[...] = own_ref[...]

    @pl.when(jnp.logical_not(mine))
    def _():
        out_ref[...] = got_ref[...]


def adam_kernel(members, parts, unread, partner_ref, own_ref, h1, h2, h3, *refs):
    count = len(parts)
    state, refs = refs[: 3 * count], refs[3 * count + unread :]
    fresh, refs = refs[: 3 * count], refs[3 * count :]
    held, made, in_sems, out_sems = refs
    loads = []
    for n, (at, width, base) in enumerate(parts):
        for k in range(3):
            src = state[3 * n + k].at[:, pl.ds(base, width)]
            loads.append((src, held.at[k, :, pl.ds(at, width)]))
    loads = fetch(loads, in_sems)
    z, mate = pair(partner_ref, members)
    use = (
        ((z == 1) & (mate == 0)) | ((z == 2) & (mate == 3)),
        ((z == 1) & (mate >= 2)) | ((z == 2) & (mate <= 1)),
        ((z == 0) & (mate != 0)) | ((z == 3) & (mate != 3)),
    )
    stores = []
    for n, (at, width, base) in enumerate(parts):
        for load in loads[3 * n : 3 * n + 3]:
            load.wait()
        for j in range(width // TILE):
            cols = slice(at + j * TILE, at + (j + 1) * TILE)
            gradient = own_ref[:, cols].astype(f32)
            for wanted, ref in zip(use, (h1, h2, h3)):
                gradient += jnp.where(wanted, ref[:, cols].astype(f32), 0.0)
            new = adam_math(held[0, :, cols], held[1, :, cols], held[2, :, cols], gradient)
            for k in range(3):
                made[k, :, cols] = new[k]
        for k in range(3):
            dst = fresh[3 * n + k].at[:, pl.ds(base, width)]
            store = pltpu.make_async_copy(made.at[k, :, pl.ds(at, width)], dst, out_sems.at[3 * n + k])
            store.start()
            stores.append(store)
    for store in stores:
        store.wait()


def return_kernel(dims, hot_ref, ret_ref, grad_ref, gate_ref):
    tok, top, rows = dims[:3]
    hidden = grad_ref.shape[1]
    hot = hot_ref[...]
    grad_ref[...] = dot(hot, ret_ref[:, :hidden], 1, 0).astype(bf16)
    gate = dot(hot, ret_ref[:, hidden:], 1, 0)[:, :1]
    spread = jnp.where(lax.shift_right_logical(iota((rows, tok), 0), log2(top)) == iota((rows, tok), 1), gate, 0.0)
    turn = ((iota((top, rows), 1) & (top - 1)) == iota((top, rows), 0)).astype(bf16)
    gate_ref[...] = dot(turn, spread.astype(bf16), 1, 0).astype(bf16)


def shape(dims, dtype=bf16):
    return jax.ShapeDtypeStruct(dims, dtype)


def per_device(
    dout,
    gates,
    saved_down_input,
    routing,
    placement,
    partner,
    frozen,
    colscale,
    adapter_down_factor,
    adapter_up_factor,
    first_moment_down,
    second_moment_down,
    first_moment_up,
    second_moment_up,
):
    groups = lax.axis_size("ep")
    members = lax.axis_size("ex")
    slots = groups * members
    tok, top = routing.shape
    model_width = dout.shape[1]
    hidden = saved_down_input.shape[2]
    rank = adapter_down_factor.shape[2]
    rows = tok * top
    cap = rows // slots
    steps = groups // 2
    block = 2 * members * cap
    dims = (tok, top, rows, slots, groups, members, cap)
    widths = chunk_widths(model_width)
    tokens = members * tok
    assert members == 4 and groups % 2 == 0

    width0 = widths[0][1]
    rest_width = model_width - width0
    hot, chunk0, rest = call(
        functools.partial(index_kernel, dims, width0),
        [shape((rows, rows)), shape((tok, width0 + rows)), shape((tok, rest_width))],
        flops=2 * rows * rows * tok,
        moved=4 * tok * model_width,
        in_specs=[HBM] * 3,
        out_specs=[VMEM] * 3,
        scratch_shapes=[pltpu.VMEM((top, tok), jnp.int32), pltpu.VMEM((1, slots), jnp.int32), DMA((4,))],
    )(routing.T, placement.reshape(1, slots), dout)

    def other_core(x):
        return lax.ppermute(x, "ep", [(i, i ^ 1) for i in range(groups)])

    def send(x, pairs):
        return lax.ppermute(x, "ex", pairs)

    got = [send(chunk0, [(i, i ^ s) for i in range(members)]) for s in range(1, members)]

    rest = tied(rest, *got)
    middle, outer = [(1, 2), (2, 1)], [(1, 0), (2, 3)]
    near = send(rest, [(0, 1), (1, 0), (2, 3), (3, 2)])
    far = send(rest, middle)
    outgoing = call(
        functools.partial(hidden_kernel, dims),
        shape((rows, hidden + LANES)),
        flops=2 * rows * rows * hidden,
        moved=4 * rows * hidden,
        in_specs=[VMEM, HBM, HBM, ANY],
        out_specs=VMEM,
        scratch_shapes=[pltpu.VMEM((top, tok), bf16), pltpu.VMEM((rows, hidden), bf16), DMA((2,))],
    )(hot, gates.T, saved_down_input.reshape(rows, hidden), near)

    arrived = lax.all_to_all(
        outgoing.reshape(slots, cap, hidden + LANES), ("ep", "ex"), split_axis=0, concat_axis=0, tiled=True
    ).reshape(rows, hidden + LANES)

    far_near = send(near, middle)
    end = send(far, outer)
    end_near = send(far_near, outer)

    own0 = call(
        functools.partial(place_direct_kernel, members),
        shape((tokens, width0 + rows)),
        moved=4 * tokens * width0,
    )(chunk0, *got)
    other0 = other_core(own0)
    pick = call(
        functools.partial(pick_kernel, dims),
        shape((rows, rows)),
        flops=2 * rows * rows * 2 * tokens,
        moved=4 * rows * rows,
        grid=(1,),
        in_specs=[pl.BlockSpec((tokens, rows), lambda i: (0, width0 // rows))] * 2,
        out_specs=pl.BlockSpec((rows, rows), lambda i: (0, 0)),
    )(own0, other0)
    down_t = adapter_down_factor[0].T
    low, gated = call(
        functools.partial(low_kernel, steps, block),
        [shape((rows, rank)), shape((rows, rank))],
        flops=2 * rows * hidden * rank,
        moved=2 * rows * hidden,
    )(arrived, down_t)

    def exchange(x, *after):
        h1 = send(x, [(0, 1), (3, 2)])
        hops = [h1]
        for hop, pairs in ((2, middle), (3, outer)):
            onward = call(
                functools.partial(onward_kernel, members, hop),
                shape(x.shape),
                moved=4 * x.size,
                in_specs=[SMEM, VMEM, VMEM] + [ANY] * len(after),
                out_specs=VMEM,
            )(partner, x, hops[-1], *after)
            hops.append(send(onward, pairs))
        return hops

    def plane_rows(c, own, other, start, *after):
        off, width = widths[c]
        blocks = call(
            functools.partial(rows_kernel, start, width, steps),
            [shape((block, width))] * steps,
            flops=2 * rows * rows * width,
            moved=4 * rows * width,
            in_specs=[VMEM] * 3 + [ANY] * len(after),
            out_specs=[VMEM] * steps,
        )(pick, own, other, *after)
        sent = [lax.ppermute(blocks[s], "ep", [(i, i ^ (2 * s)) for i in range(groups)]) for s in range(1, steps)]
        return [blocks[0]] + sent

    def up_grad(blocks, *after):
        out = shape((rank, blocks[0].shape[1]))
        return call(
            functools.partial(up_grad_kernel, steps),
            out,
            flops=2 * rows * rank * out.shape[1],
            in_specs=[VMEM] * (steps + 1) + [ANY] * len(after),
            out_specs=VMEM,
        )(*blocks, gated, *after)

    def expert(c, blocks, after, *carry):
        off, width = widths[c]
        tiles = width // TILE
        final = c == len(widths) - 1
        args = list(blocks) + [frozen[0], colscale, adapter_up_factor[0]] + list(after) + list(carry)
        specs = [VMEM] * steps + [HBM] * 3 + [ANY] * len(after) + [VMEM] * len(carry)
        scratch = []
        if final:
            args += [gated, arrived, down_t, low]
            specs += [VMEM] * 4
            outs = [shape((rank, width + hidden)), shape((rows, hidden + LANES))]
            scratch = [pltpu.VMEM((rows, hidden), f32), pltpu.VMEM((rows, rank), f32)]
        else:
            outs = [shape((rows, hidden), f32), shape((rows, rank), f32)]
        scratch += [
            pltpu.VMEM((tiles, hidden, TILE), bf16),
            pltpu.VMEM((1, width), f32),
            pltpu.VMEM((rank, width), bf16),
            DMA((tiles + 2,)),
        ]
        return call(
            functools.partial(expert_kernel, steps, off, len(after), not carry, final),
            outs,
            flops=2 * rows * hidden * width,
            moved=2 * hidden * width + 2 * rows * width,
            limit=EXPERT_VMEM_LIMIT,
            in_specs=specs,
            out_specs=[VMEM] * len(outs),
            scratch_shapes=scratch,
        )(*args)

    def adam(grad, hops, parts, states, before, *after):
        total = sum(width for _, width, _ in parts)
        arrays = [x for state in states for x in state]
        carried = len(before)
        return call(
            functools.partial(adam_kernel, members, parts, carried + len(after)),
            [shape(x.shape) for x in arrays],
            flops=20 * rank * total,
            moved=20 * rank * total,
            limit=EXPERT_VMEM_LIMIT,
            in_specs=[SMEM] + [VMEM] * 4 + [HBM] * (len(arrays) + carried) + [ANY] * len(after),
            out_specs=[HBM] * len(arrays),
            input_output_aliases={5 + len(arrays) + i: i for i in range(carried)},
            scratch_shapes=[pltpu.VMEM((3, rank, total), bf16)] * 2 + [DMA((len(arrays),))] * 2,
        )(partner, grad, *hops, *arrays, *before, *after)

    up_state = [adapter_up_factor[0], first_moment_up[0], second_moment_up[0]]
    down_state = [down_t, first_moment_down[0].T, second_moment_down[0].T]
    (_, _), (off1, width1), (off2, width2) = widths

    blocks0 = plane_rows(0, own0, other0, 0)
    carry = expert(0, blocks0, [])
    grad0 = up_grad(blocks0)
    own1 = call(
        place_relay_kernel,
        shape((tokens, rest_width)),
        moved=4 * tokens * rest_width,
        in_specs=[VMEM] * 6 + [ANY] * 2,
        out_specs=VMEM,
    )(rest, near, far, far_near, end, end_near, carry[0], grad0)
    other1 = other_core(own1)
    blocks1 = plane_rows(1, own1, other1, 0)
    blocks2 = plane_rows(2, own1, other1, width1, blocks1[0])
    hops0 = exchange(grad0, blocks2[0])
    grad1 = up_grad(blocks1, hops0[1])
    carry = expert(1, blocks1, [blocks2[0]], *carry)
    grad2, ret = expert(2, blocks2, [grad1, hops0[2]], *carry)
    hops1 = exchange(grad1, ret)
    hops2 = exchange(grad2)
    fresh_up = adam(grad0, hops0, [(0, width0, 0)], [up_state], [], ret)
    fresh_up = adam(grad1, hops1, [(0, width1, off1)], [up_state], fresh_up)
    fresh = adam(grad2, hops2, [(0, width2, off2), (width2, hidden, 0)], [up_state, down_state], fresh_up)
    fresh_up, fresh_down = fresh[:3], fresh[3:]

    returned = lax.all_to_all(
        ret.reshape(slots, cap, hidden + LANES), ("ep", "ex"), split_axis=0, concat_axis=0, tiled=True
    ).reshape(rows, hidden + LANES)
    row_grad, gate_grad = call(
        functools.partial(return_kernel, dims),
        [shape((rows, hidden)), shape((top, tok))],
        flops=2 * rows * rows * hidden,
        moved=4 * rows * hidden,
    )(hot, returned)

    return (
        row_grad.reshape(tok, top, hidden),
        gate_grad.T,
        fresh_down[0].T[None],
        fresh_up[0][None],
        fresh_down[1].T[None],
        fresh_down[2].T[None],
        fresh_up[1][None],
        fresh_up[2][None],
    )


def solution(mesh):
    two = P(("ep", "ex"), None)
    three = P(("ep", "ex"), None, None)
    return jax.shard_map(
        per_device,
        mesh=mesh,
        in_specs=(two, two, three, two, P(), P(), three, two) + (three,) * 6,
        out_specs=(three, two) + (three,) * 6,
        check_vma=False,
    )
```

```python
import functools

import jax
import jax.numpy as jnp
from jax import lax
from jax.experimental import pallas as pl
from jax.experimental.pallas import tpu as pltpu
from jax.sharding import PartitionSpec as P

adapter_scale = 2.0
beta_one = 0.9
beta_two = 0.999
adam_eps = 1e-08
learn_rate = 0.01
weight_decay = 0.01
adam_step = 10

TILE = 512
LANES = 128
SHARES = (5, 6, 3)
VMEM_LIMIT = 24 * 1024 * 1024
EXPERT_VMEM_LIMIT = 44 * 1024 * 1024
bf16 = jnp.bfloat16
f32 = jnp.float32


def chunk_widths(width):
    tiles = width // TILE
    total = sum(SHARES)
    edges = [0]
    taken = 0
    for share in SHARES:
        taken += share
        edges.append(tiles * taken // total)
    return [(edges[i] * TILE, (edges[i + 1] - edges[i]) * TILE) for i in range(len(SHARES)) if edges[i + 1] > edges[i]]


def log2(n):
    k = n.bit_length() - 1
    assert 1 << k == n
    return k


def iota(shape, dim):
    return lax.broadcasted_iota(jnp.int32, shape, dim)


def dot(a, b, ca, cb):
    return lax.dot_general(a, b, (((ca,), (cb,)), ((), ())), preferred_element_type=f32)


HBM = pl.BlockSpec(memory_space=pltpu.HBM)
VMEM = pl.BlockSpec(memory_space=pltpu.VMEM)
SMEM = pl.BlockSpec(memory_space=pltpu.SMEM)
ANY = pl.BlockSpec(memory_space=pl.ANY)
DMA = pltpu.SemaphoreType.DMA


def fetch(pairs, sems):
    copies = [pltpu.make_async_copy(src, dst, sems.at[i]) for i, (src, dst) in enumerate(pairs)]
    for copy in copies:
        copy.start()
    return copies


def call(kernel, outs, flops=0, moved=0, limit=VMEM_LIMIT, **kw):
    params = pltpu.CompilerParams(vmem_limit_bytes=limit)
    cost = pl.CostEstimate(flops=flops, bytes_accessed=moved, transcendentals=0)
    return pl.pallas_call(kernel, out_shape=outs, compiler_params=params, cost_estimate=cost, **kw)


def index_kernel(dims, width, rout_hbm, place_hbm, dout_hbm, hot_ref, chunk_ref, rest_ref, rout_ref, place_ref, sems):
    rest_width = rest_ref.shape[1]
    copies = fetch(
        [
            (rout_hbm, rout_ref),
            (place_hbm, place_ref),
            (dout_hbm.at[:, pl.ds(0, width)], chunk_ref.at[:, pl.ds(0, width)]),
            (dout_hbm.at[:, pl.ds(width, rest_width)], rest_ref),
        ],
        sems,
    )
    copies[0].wait()
    copies[1].wait()
    tok, top, rows, slots, groups, members, cap = dims
    kt = log2(top)
    rid_c, rid_r = iota((rows, 1), 0), iota((1, rows), 1)
    spread = (lax.shift_right_logical(iota((rows, tok), 0), kt) == iota((rows, tok), 1)).astype(bf16)
    routes = rout_ref[...].astype(f32).astype(bf16)
    wide = dot(spread, routes, 1, 1)
    e_col = jnp.sum(jnp.where((iota((rows, top), 0) & (top - 1)) == iota((rows, top), 1), wide, 0.0), axis=1, keepdims=True)
    tall = dot(routes, spread, 1, 1)
    e_row = jnp.sum(jnp.where((iota((top, rows), 1) & (top - 1)) == iota((top, rows), 0), tall, 0.0), axis=0, keepdims=True)
    earlier = rid_r < rid_c
    turn = jnp.sum(jnp.where((e_col == e_row) & earlier, 1.0, 0.0), axis=1, keepdims=True).astype(jnp.int32)
    holds = e_col == place_ref[...].astype(f32)
    slot = iota((rows, slots), 1).astype(f32)
    first = jnp.min(jnp.where(holds, slot, float(slots)), axis=1, keepdims=True)
    last = jnp.max(jnp.where(holds, slot, -1.0), axis=1, keepdims=True)
    target = jnp.where((turn & 1) == 1, last, first)
    target_row = jnp.sum(jnp.where(rid_c == rid_r, target, 0.0), axis=0, keepdims=True)
    pos = jnp.sum(jnp.where((target == target_row) & earlier, 1.0, 0.0), axis=1, keepdims=True).astype(jnp.int32)
    target = target.astype(jnp.int32)
    place = target * cap + pos
    place_z = ((target & (members - 1)) * groups + lax.shift_right_logical(target, log2(members))) * cap + pos
    hot_ref[...] = (place == rid_r).astype(f32).astype(bf16)
    hot_z = (place_z == rid_r).astype(f32).astype(bf16)
    chunk_ref[:, width:] = dot(spread, hot_z, 0, 0).astype(bf16)
    copies[2].wait()
    copies[3].wait()


def tied_kernel(*refs):
    pass


def tied(x, *after):
    return call(
        tied_kernel,
        shape(x.shape),
        in_specs=[ANY] * (1 + len(after)),
        out_specs=ANY,
        input_output_aliases={0: 0},
    )(x, *after)


def hidden_kernel(dims, hot_ref, gate_hbm, hidden_hbm, after_ref, out_ref, gate_ref, hidden_ref, sems):
    tok, top, rows = dims[:3]
    copies = fetch([(gate_hbm, gate_ref), (hidden_hbm, hidden_ref)], sems)
    copies[0].wait()
    width = hidden_ref.shape[1]
    hot = hot_ref[...]
    spread = (lax.shift_right_logical(iota((rows, tok), 0), log2(top)) == iota((rows, tok), 1)).astype(bf16)
    wide = dot(spread, gate_ref[...], 1, 1)
    gate = jnp.sum(jnp.where((iota((rows, top), 0) & (top - 1)) == iota((rows, top), 1), wide, 0.0), axis=1, keepdims=True)
    out_ref[:, width:] = dot(hot, jnp.broadcast_to(gate, (rows, LANES)).astype(bf16), 0, 0).astype(bf16)
    copies[1].wait()
    out_ref[:, :width] = dot(hot, hidden_ref[...], 0, 0).astype(bf16)


def place_direct_kernel(members, *refs):
    out_ref = refs[-1]
    me = lax.axis_index("ex")
    tok = refs[0].shape[0]
    for s in range(members):
        out_ref[pl.ds(pl.multiple_of((me ^ s) * tok, tok), tok), :] = refs[s][...]


def place_relay_kernel(own, near, far, far_near, end, end_near, *refs):
    out_ref = refs[-1]
    me = lax.axis_index("ex")
    tok = own.shape[0]
    orders = (
        (own, near, end, end_near),
        (near, own, far, far_near),
        (far_near, far, own, near),
        (end_near, end, near, own),
    )
    for z, order in enumerate(orders):

        @pl.when(me == z)
        def _():
            for i, ref in enumerate(order):
                out_ref[i * tok : (i + 1) * tok, :] = ref[...]


def pick_kernel(dims, own_ref, other_ref, pick_ref):
    tok, top, rows, slots, groups, members, cap = dims
    tokens = members * tok
    ep, z = lax.axis_index("ep"), lax.axis_index("ex")
    chip, core = lax.shift_right_logical(ep, 1), ep & 1
    row, q = iota((rows, rows), 0), iota((rows, rows), 1)
    p = row & (cap - 1)
    step = lax.shift_right_logical(row, log2(2 * members * cap))
    wanted = (z * groups + (step ^ chip) * 2 + core) * cap + p
    choose = (wanted == q).astype(f32).astype(bf16)
    for b, ref in enumerate((own_ref, other_ref)):
        found = dot(choose, ref[...], 1, 1)
        r = iota((rows, tokens), 0)
        from_core = lax.shift_right_logical(r, log2(members * cap)) & 1
        from_z = lax.shift_right_logical(r, log2(cap)) & (members - 1)
        t = lax.shift_right_logical(iota((rows, tokens), 1), log2(tok))
        keep = (from_core == (core ^ b)) & (from_z == t)
        pick_ref[:, b * tokens : (b + 1) * tokens] = jnp.where(keep, found, 0.0).astype(bf16)


def rows_kernel(start, width, steps, pick_ref, own_ref, other_ref, *out_refs):
    out_refs = out_refs[-steps:]
    tokens = own_ref.shape[0]
    block = out_refs[0].shape[0]
    pick = pick_ref[...]
    for j in range(width // TILE):
        cols = slice(j * TILE, (j + 1) * TILE)
        took = slice(start + j * TILE, start + (j + 1) * TILE)
        got = dot(pick[:, :tokens], own_ref[:, took], 1, 0) + dot(pick[:, tokens:], other_ref[:, took], 1, 0)
        for s, ref in enumerate(out_refs):
            ref[:, cols] = got[s * block : (s + 1) * block].astype(bf16)


def order_by_step(ref, steps, block, cols):
    chip = lax.shift_right_logical(lax.axis_index("ep"), 1)
    return jnp.concatenate(
        [ref[pl.ds(pl.multiple_of((chip ^ s) * block, block), block), cols] for s in range(steps)], axis=0
    )


def low_kernel(steps, block, arrived_ref, down_ref, low_ref, gated_ref):
    hidden = down_ref.shape[1]
    rows = order_by_step(arrived_ref, steps, block, slice(0, hidden))
    gate = order_by_step(arrived_ref, steps, block, slice(hidden, hidden + LANES))[:, :1].astype(f32)
    low = dot(rows, down_ref[...], 1, 1).astype(bf16)
    low_ref[...] = low
    gated_ref[...] = (adapter_scale * gate * low.astype(f32)).astype(bf16)


def up_grad_kernel(steps, *refs):
    blocks, gated_ref, out_ref = refs[:steps], refs[steps], refs[-1]
    for j in range(out_ref.shape[1] // TILE):
        cols = slice(j * TILE, (j + 1) * TILE)
        rows = jnp.concatenate([b[:, cols] for b in blocks], axis=0)
        out_ref[:, cols] = dot(gated_ref[...], rows, 0, 0).astype(bf16)


def expert_kernel(steps, off, unread, first, final, *refs):
    blocks = refs[:steps]
    width = blocks[0].shape[1]
    tiles = width // TILE
    refs = refs[steps:]
    frozen_hbm, scale_hbm, up_hbm = refs[:3]
    refs = refs[3 + unread :]
    frozen_ref, scale_ref, up_ref, sems = refs[-4:]
    refs = refs[:-4]
    copies = fetch(
        [(scale_hbm.at[:, pl.ds(off, width)], scale_ref)]
        + [(frozen_hbm.at[:, pl.ds(off + j * TILE, TILE)], frozen_ref.at[j]) for j in range(tiles)]
        + [(up_hbm.at[:, pl.ds(off, width)], up_ref)],
        sems,
    )
    if not first:
        back_in, low_in = refs[:2]
        refs = refs[2:]
    if final:
        gated_ref, arrived_ref, down_ref, low_ref = refs[:4]
        up_grad_ref, ret_ref, back_ref, thin_ref = refs[4:]
        for j in range(tiles):
            cols = slice(j * TILE, (j + 1) * TILE)
            rows = jnp.concatenate([b[:, cols] for b in blocks], axis=0)
            up_grad_ref[:, cols] = dot(gated_ref[...], rows, 0, 0).astype(bf16)
    else:
        back_ref, thin_ref = refs
    copies[0].wait()
    for j in range(tiles):
        cols = slice(j * TILE, (j + 1) * TILE)
        rows = jnp.concatenate([b[:, cols] for b in blocks], axis=0)
        scaled = (rows.astype(f32) * scale_ref[:, cols]).astype(bf16)
        copies[1 + j].wait()
        part = dot(scaled, frozen_ref[j], 1, 1)
        if j > 0:
            part += back_ref[...]
        elif not first:
            part += back_in[...]
        back_ref[...] = part
    copies[1 + tiles].wait()
    thin = dot(jnp.concatenate([b[...] for b in blocks], axis=0), up_ref[...], 1, 1)
    thin_ref[...] = thin if first else thin + low_in[...]
    if final:
        block = blocks[0].shape[0]
        hidden = down_ref.shape[1]
        chip = lax.shift_right_logical(lax.axis_index("ep"), 1)
        saved = order_by_step(arrived_ref, steps, block, slice(0, hidden))
        gate = order_by_step(arrived_ref, steps, block, slice(hidden, hidden + LANES))[:, :1].astype(f32)
        back = back_ref[...]
        thin = thin_ref[...]
        back_low = (gate * thin).astype(bf16)
        grad = (gate * back + adapter_scale * dot(back_low, down_ref[...], 1, 0)).astype(bf16)
        gate_grad = jnp.sum(saved.astype(f32) * back, axis=1, keepdims=True) + adapter_scale * jnp.sum(
            low_ref[...].astype(f32) * thin, axis=1, keepdims=True
        )
        gate_grad = jnp.broadcast_to(gate_grad, (gate_grad.shape[0], LANES)).astype(bf16)
        for s in range(steps):
            at = pl.ds(pl.multiple_of((chip ^ s) * block, block), block)
            ret_ref[at, :hidden] = grad[s * block : (s + 1) * block]
            ret_ref[at, hidden:] = gate_grad[s * block : (s + 1) * block]
        up_grad_ref[:, width:] = (adapter_scale * dot(back_low, saved, 0, 0)).astype(bf16)


def adam_math(weights, moment, second_moment, gradient):
    weights_wide = weights.astype(f32)
    first = beta_one * moment.astype(f32) + (1.0 - beta_one) * gradient
    second = beta_two * second_moment.astype(f32) + (1.0 - beta_two) * gradient * gradient
    first_hat = first * (1.0 / (1.0 - beta_one**adam_step))
    second_hat = second * (1.0 / (1.0 - beta_two**adam_step))
    fresh = weights_wide - learn_rate * (
        first_hat / (jnp.sqrt(second_hat) + adam_eps) + weight_decay * weights_wide
    )
    return (fresh.astype(bf16), first.astype(bf16), second.astype(bf16))


def pair(partner_ref, members):
    z = lax.axis_index("ex")
    return z, partner_ref[lax.axis_index("ep") * members + z] & (members - 1)


def onward_kernel(members, hop, partner_ref, own_ref, got_ref, *refs):
    out_ref = refs[-1]
    z, mate = pair(partner_ref, members)
    if hop == 2:
        mine = ((z == 1) & (mate >= 2)) | ((z == 2) & (mate <= 1))
    else:
        mine = ((z == 1) & (mate == 0)) | ((z == 2) & (mate == 3))

    @pl.when(mine)
    def _():
        out_ref[...] = own_ref[...]

    @pl.when(jnp.logical_not(mine))
    def _():
        out_ref[...] = got_ref[...]


def adam_kernel(members, parts, unread, partner_ref, own_ref, h1, h2, h3, *refs):
    count = len(parts)
    state, refs = refs[: 3 * count], refs[3 * count + unread :]
    fresh, refs = refs[: 3 * count], refs[3 * count :]
    held, made, in_sems, out_sems = refs
    loads = []
    for n, (at, width, base) in enumerate(parts):
        for k in range(3):
            src = state[3 * n + k].at[:, pl.ds(base, width)]
            loads.append((src, held.at[k, :, pl.ds(at, width)]))
    loads = fetch(loads, in_sems)
    z, mate = pair(partner_ref, members)
    use = (
        ((z == 1) & (mate == 0)) | ((z == 2) & (mate == 3)),
        ((z == 1) & (mate >= 2)) | ((z == 2) & (mate <= 1)),
        ((z == 0) & (mate != 0)) | ((z == 3) & (mate != 3)),
    )
    stores = []
    for n, (at, width, base) in enumerate(parts):
        for load in loads[3 * n : 3 * n + 3]:
            load.wait()
        for j in range(width // TILE):
            cols = slice(at + j * TILE, at + (j + 1) * TILE)
            gradient = own_ref[:, cols].astype(f32)
            for wanted, ref in zip(use, (h1, h2, h3)):
                gradient += jnp.where(wanted, ref[:, cols].astype(f32), 0.0)
            new = adam_math(held[0, :, cols], held[1, :, cols], held[2, :, cols], gradient)
            for k in range(3):
                made[k, :, cols] = new[k]
        for k in range(3):
            dst = fresh[3 * n + k].at[:, pl.ds(base, width)]
            store = pltpu.make_async_copy(made.at[k, :, pl.ds(at, width)], dst, out_sems.at[3 * n + k])
            store.start()
            stores.append(store)
    for store in stores:
        store.wait()


def return_kernel(dims, hot_ref, ret_ref, grad_ref, gate_ref):
    tok, top, rows = dims[:3]
    hidden = grad_ref.shape[1]
    hot = hot_ref[...]
    grad_ref[...] = dot(hot, ret_ref[:, :hidden], 1, 0).astype(bf16)
    gate = dot(hot, ret_ref[:, hidden:], 1, 0)[:, :1]
    spread = jnp.where(lax.shift_right_logical(iota((rows, tok), 0), log2(top)) == iota((rows, tok), 1), gate, 0.0)
    turn = ((iota((top, rows), 1) & (top - 1)) == iota((top, rows), 0)).astype(bf16)
    gate_ref[...] = dot(turn, spread.astype(bf16), 1, 0).astype(bf16)


def shape(dims, dtype=bf16):
    return jax.ShapeDtypeStruct(dims, dtype)


def per_device(
    dout,
    gates,
    saved_down_input,
    routing,
    placement,
    partner,
    frozen,
    colscale,
    adapter_down_factor,
    adapter_up_factor,
    first_moment_down,
    second_moment_down,
    first_moment_up,
    second_moment_up,
):
    groups = lax.axis_size("ep")
    members = lax.axis_size("ex")
    slots = groups * members
    tok, top = routing.shape
    model_width = dout.shape[1]
    hidden = saved_down_input.shape[2]
    rank = adapter_down_factor.shape[2]
    rows = tok * top
    cap = rows // slots
    steps = groups // 2
    block = 2 * members * cap
    dims = (tok, top, rows, slots, groups, members, cap)
    widths = chunk_widths(model_width)
    tokens = members * tok
    assert members == 4 and groups % 2 == 0

    width0 = widths[0][1]
    rest_width = model_width - width0
    hot, chunk0, rest = call(
        functools.partial(index_kernel, dims, width0),
        [shape((rows, rows)), shape((tok, width0 + rows)), shape((tok, rest_width))],
        flops=2 * rows * rows * tok,
        moved=4 * tok * model_width,
        in_specs=[HBM] * 3,
        out_specs=[VMEM] * 3,
        scratch_shapes=[pltpu.VMEM((top, tok), jnp.int32), pltpu.VMEM((1, slots), jnp.int32), DMA((4,))],
    )(routing.T, placement.reshape(1, slots), dout)

    def other_core(x):
        return lax.ppermute(x, "ep", [(i, i ^ 1) for i in range(groups)])

    def send(x, pairs):
        return lax.ppermute(x, "ex", pairs)

    got = [send(chunk0, [(i, i ^ s) for i in range(members)]) for s in range(1, members)]

    rest = tied(rest, *got)
    middle, outer = [(1, 2), (2, 1)], [(1, 0), (2, 3)]
    near = send(rest, [(0, 1), (1, 0), (2, 3), (3, 2)])
    far = send(rest, middle)
    far_near = send(near, middle)
    end = send(far, outer)
    end_near = send(far_near, outer)

    own0 = call(
        functools.partial(place_direct_kernel, members),
        shape((tokens, width0 + rows)),
        moved=4 * tokens * width0,
    )(chunk0, *got)
    other0 = other_core(own0)
    pick = call(
        functools.partial(pick_kernel, dims),
        shape((rows, rows)),
        flops=2 * rows * rows * 2 * tokens,
        moved=4 * rows * rows,
        grid=(1,),
        in_specs=[pl.BlockSpec((tokens, rows), lambda i: (0, width0 // rows))] * 2,
        out_specs=pl.BlockSpec((rows, rows), lambda i: (0, 0)),
    )(own0, other0)
    down_t = adapter_down_factor[0].T

    def onward(hop, x, got, *after):
        moved = call(
            functools.partial(onward_kernel, members, hop),
            shape(x.shape),
            moved=4 * x.size,
            in_specs=[SMEM, VMEM, VMEM] + [ANY] * len(after),
            out_specs=VMEM,
        )(partner, x, got, *after)
        return send(moved, middle if hop == 2 else outer)

    def first_hop(x):
        return send(x, [(0, 1), (3, 2)])

    def plane_rows(c, own, other, start, *after):
        off, width = widths[c]
        blocks = call(
            functools.partial(rows_kernel, start, width, steps),
            [shape((block, width))] * steps,
            flops=2 * rows * rows * width,
            moved=4 * rows * width,
            in_specs=[VMEM] * 3 + [ANY] * len(after),
            out_specs=[VMEM] * steps,
        )(pick, own, other, *after)
        sent = [lax.ppermute(blocks[s], "ep", [(i, i ^ (2 * s)) for i in range(groups)]) for s in range(1, steps)]
        return [blocks[0]] + sent

    def up_grad(blocks, *after):
        out = shape((rank, blocks[0].shape[1]))
        return call(
            functools.partial(up_grad_kernel, steps),
            out,
            flops=2 * rows * rank * out.shape[1],
            in_specs=[VMEM] * (steps + 1) + [ANY] * len(after),
            out_specs=VMEM,
        )(*blocks, gated, *after)

    def expert(c, blocks, after, *carry):
        off, width = widths[c]
        tiles = width // TILE
        final = c == len(widths) - 1
        args = list(blocks) + [frozen[0], colscale, adapter_up_factor[0]] + list(after) + list(carry)
        specs = [VMEM] * steps + [HBM] * 3 + [ANY] * len(after) + [VMEM] * len(carry)
        scratch = []
        if final:
            args += [gated, arrived, down_t, low]
            specs += [VMEM] * 4
            outs = [shape((rank, width + hidden)), shape((rows, hidden + LANES))]
            scratch = [pltpu.VMEM((rows, hidden), f32), pltpu.VMEM((rows, rank), f32)]
        else:
            outs = [shape((rows, hidden), f32), shape((rows, rank), f32)]
        scratch += [
            pltpu.VMEM((tiles, hidden, TILE), bf16),
            pltpu.VMEM((1, width), f32),
            pltpu.VMEM((rank, width), bf16),
            DMA((tiles + 2,)),
        ]
        return call(
            functools.partial(expert_kernel, steps, off, len(after), not carry, final),
            outs,
            flops=2 * rows * hidden * width,
            moved=2 * hidden * width + 2 * rows * width,
            limit=EXPERT_VMEM_LIMIT,
            in_specs=specs,
            out_specs=[VMEM] * len(outs),
            scratch_shapes=scratch,
        )(*args)

    def adam(grad, hops, parts, states, before, *after):
        total = sum(width for _, width, _ in parts)
        arrays = [x for state in states for x in state]
        carried = len(before)
        return call(
            functools.partial(adam_kernel, members, parts, carried + len(after)),
            [shape(x.shape) for x in arrays],
            flops=20 * rank * total,
            moved=20 * rank * total,
            limit=EXPERT_VMEM_LIMIT,
            in_specs=[SMEM] + [VMEM] * 4 + [HBM] * (len(arrays) + carried) + [ANY] * len(after),
            out_specs=[HBM] * len(arrays),
            input_output_aliases={5 + len(arrays) + i: i for i in range(carried)},
            scratch_shapes=[pltpu.VMEM((3, rank, total), bf16)] * 2 + [DMA((len(arrays),))] * 2,
        )(partner, grad, *hops, *arrays, *before, *after)

    up_state = [adapter_up_factor[0], first_moment_up[0], second_moment_up[0]]
    down_state = [down_t, first_moment_down[0].T, second_moment_down[0].T]
    (_, _), (off1, width1), (off2, width2) = widths

    blocks0 = plane_rows(0, own0, other0, 0)
    outgoing = call(
        functools.partial(hidden_kernel, dims),
        shape((rows, hidden + LANES)),
        flops=2 * rows * rows * hidden,
        moved=4 * rows * hidden,
        in_specs=[VMEM, HBM, HBM, ANY],
        out_specs=VMEM,
        scratch_shapes=[pltpu.VMEM((top, tok), bf16), pltpu.VMEM((rows, hidden), bf16), DMA((2,))],
    )(hot, gates.T, saved_down_input.reshape(rows, hidden), blocks0[0])

    arrived = lax.all_to_all(
        outgoing.reshape(slots, cap, hidden + LANES), ("ep", "ex"), split_axis=0, concat_axis=0, tiled=True
    ).reshape(rows, hidden + LANES)

    low, gated = call(
        functools.partial(low_kernel, steps, block),
        [shape((rows, rank)), shape((rows, rank))],
        flops=2 * rows * hidden * rank,
        moved=2 * rows * hidden,
    )(arrived, down_t)

    own1 = call(
        place_relay_kernel,
        shape((tokens, rest_width)),
        moved=4 * tokens * rest_width,
        in_specs=[VMEM] * 6 + [ANY] * steps,
        out_specs=VMEM,
    )(rest, near, far, far_near, end, end_near, outgoing, *blocks0[1:])
    other1 = other_core(own1)
    blocks1 = plane_rows(1, own1, other1, 0)
    blocks2 = plane_rows(2, own1, other1, width1, blocks1[0])
    grad0 = up_grad(blocks0, blocks2[0])
    carry0 = expert(0, blocks0, [grad0])
    grad1 = up_grad(blocks1, carry0[0])
    first0 = first_hop(grad0)
    first1 = first_hop(grad1)
    second0 = onward(2, grad0, first0, grad1)
    carry1 = expert(1, blocks1, [grad1], *carry0)
    grad2, ret = expert(2, blocks2, [carry1[0], second0, first1], *carry1)
    third0 = onward(3, grad0, second0, carry1[0])
    second1 = onward(2, grad1, first1, carry1[0])
    first2 = first_hop(grad2)
    returned = lax.all_to_all(
        ret.reshape(slots, cap, hidden + LANES), ("ep", "ex"), split_axis=0, concat_axis=0, tiled=True
    ).reshape(rows, hidden + LANES)
    third1 = onward(3, grad1, second1, ret)
    fresh_up = adam(grad0, (first0, second0, third0), [(0, width0, 0)], [up_state], [], ret)
    second2 = onward(2, grad2, first2, ret)
    row_grad, gate_grad = call(
        functools.partial(return_kernel, dims),
        [shape((rows, hidden)), shape((top, tok))],
        flops=2 * rows * rows * hidden,
        moved=4 * rows * hidden,
    )(hot, returned)
    third2 = onward(3, grad2, second2, row_grad, fresh_up[0])
    fresh_up = adam(grad1, (first1, second1, third1), [(0, width1, off1)], [up_state], fresh_up)
    fresh = adam(
        grad2,
        (first2, second2, third2),
        [(0, width2, off2), (width2, hidden, 0)],
        [up_state, down_state],
        fresh_up,
    )
    fresh_up, fresh_down = fresh[:3], fresh[3:]

    return (
        row_grad.reshape(tok, top, hidden),
        gate_grad.T,
        fresh_down[0].T[None],
        fresh_up[0][None],
        fresh_down[1].T[None],
        fresh_down[2].T[None],
        fresh_up[1][None],
        fresh_up[2][None],
    )


def solution(mesh):
    two = P(("ep", "ex"), None)
    three = P(("ep", "ex"), None, None)
    return jax.shard_map(
        per_device,
        mesh=mesh,
        in_specs=(two, two, three, two, P(), P(), three, two) + (three,) * 6,
        out_specs=(three, two) + (three,) * 6,
        check_vma=False,
    )
```

```python
import functools

import jax
import jax.numpy as jnp
from jax import lax
from jax.experimental import pallas as pl
from jax.experimental.pallas import tpu as pltpu
from jax.sharding import PartitionSpec as P

adapter_scale = 2.0
beta_one = 0.9
beta_two = 0.999
adam_eps = 1e-08
learn_rate = 0.01
weight_decay = 0.01
adam_step = 10

TILE = 512
LANES = 128
SHARES = (5, 6, 3)
VMEM_LIMIT = 24 * 1024 * 1024
EXPERT_VMEM_LIMIT = 42 * 1024 * 1024
bf16 = jnp.bfloat16
f32 = jnp.float32


def chunk_widths(width):
    tiles = width // TILE
    total = sum(SHARES)
    edges = [0]
    taken = 0
    for share in SHARES:
        taken += share
        edges.append(tiles * taken // total)
    return [(edges[i] * TILE, (edges[i + 1] - edges[i]) * TILE) for i in range(len(SHARES)) if edges[i + 1] > edges[i]]


def log2(n):
    k = n.bit_length() - 1
    assert 1 << k == n
    return k


def iota(shape, dim):
    return lax.broadcasted_iota(jnp.int32, shape, dim)


def dot(a, b, ca, cb):
    return lax.dot_general(a, b, (((ca,), (cb,)), ((), ())), preferred_element_type=f32)


HBM = pl.BlockSpec(memory_space=pltpu.HBM)
VMEM = pl.BlockSpec(memory_space=pltpu.VMEM)
SMEM = pl.BlockSpec(memory_space=pltpu.SMEM)
ANY = pl.BlockSpec(memory_space=pl.ANY)
DMA = pltpu.SemaphoreType.DMA


def fetch(pairs, sems):
    copies = [pltpu.make_async_copy(src, dst, sems.at[i]) for i, (src, dst) in enumerate(pairs)]
    for copy in copies:
        copy.start()
    return copies


def call(kernel, outs, flops=0, moved=0, limit=VMEM_LIMIT, **kw):
    params = pltpu.CompilerParams(vmem_limit_bytes=limit)
    cost = pl.CostEstimate(flops=flops, bytes_accessed=moved, transcendentals=0)
    return pl.pallas_call(kernel, out_shape=outs, compiler_params=params, cost_estimate=cost, **kw)


def index_kernel(dims, width, rout_hbm, place_hbm, dout_hbm, hot_ref, chunk_ref, rest_ref, rout_ref, place_ref, sems):
    rest_width = rest_ref.shape[1]
    copies = fetch(
        [
            (rout_hbm, rout_ref),
            (place_hbm, place_ref),
            (dout_hbm.at[:, pl.ds(0, width)], chunk_ref.at[:, pl.ds(0, width)]),
            (dout_hbm.at[:, pl.ds(width, rest_width)], rest_ref),
        ],
        sems,
    )
    copies[0].wait()
    copies[1].wait()
    tok, top, rows, slots, groups, members, cap = dims
    kt = log2(top)
    rid_c, rid_r = iota((rows, 1), 0), iota((1, rows), 1)
    spread = (lax.shift_right_logical(iota((rows, tok), 0), kt) == iota((rows, tok), 1)).astype(bf16)
    routes = rout_ref[...].astype(f32).astype(bf16)
    wide = dot(spread, routes, 1, 1)
    e_col = jnp.sum(jnp.where((iota((rows, top), 0) & (top - 1)) == iota((rows, top), 1), wide, 0.0), axis=1, keepdims=True)
    tall = dot(routes, spread, 1, 1)
    e_row = jnp.sum(jnp.where((iota((top, rows), 1) & (top - 1)) == iota((top, rows), 0), tall, 0.0), axis=0, keepdims=True)
    earlier = rid_r < rid_c
    turn = jnp.sum(jnp.where((e_col == e_row) & earlier, 1.0, 0.0), axis=1, keepdims=True).astype(jnp.int32)
    holds = e_col == place_ref[...].astype(f32)
    slot = iota((rows, slots), 1).astype(f32)
    first = jnp.min(jnp.where(holds, slot, float(slots)), axis=1, keepdims=True)
    last = jnp.max(jnp.where(holds, slot, -1.0), axis=1, keepdims=True)
    target = jnp.where((turn & 1) == 1, last, first)
    target_row = jnp.sum(jnp.where(rid_c == rid_r, target, 0.0), axis=0, keepdims=True)
    pos = jnp.sum(jnp.where((target == target_row) & earlier, 1.0, 0.0), axis=1, keepdims=True).astype(jnp.int32)
    target = target.astype(jnp.int32)
    place = target * cap + pos
    place_z = ((target & (members - 1)) * groups + lax.shift_right_logical(target, log2(members))) * cap + pos
    hot_ref[...] = (place == rid_r).astype(f32).astype(bf16)
    hot_z = (place_z == rid_r).astype(f32).astype(bf16)
    chunk_ref[:, width:] = dot(spread, hot_z, 0, 0).astype(bf16)
    copies[2].wait()
    copies[3].wait()


def tied_kernel(*refs):
    pass


def tied(x, *after):
    return call(
        tied_kernel,
        shape(x.shape),
        in_specs=[ANY] * (1 + len(after)),
        out_specs=ANY,
        input_output_aliases={0: 0},
    )(x, *after)


def hidden_kernel(dims, hot_ref, gate_hbm, hidden_hbm, after_ref, out_ref, gate_ref, hidden_ref, sems):
    tok, top, rows = dims[:3]
    copies = fetch([(gate_hbm, gate_ref), (hidden_hbm, hidden_ref)], sems)
    copies[0].wait()
    width = hidden_ref.shape[1]
    hot = hot_ref[...]
    spread = (lax.shift_right_logical(iota((rows, tok), 0), log2(top)) == iota((rows, tok), 1)).astype(bf16)
    wide = dot(spread, gate_ref[...], 1, 1)
    gate = jnp.sum(jnp.where((iota((rows, top), 0) & (top - 1)) == iota((rows, top), 1), wide, 0.0), axis=1, keepdims=True)
    out_ref[:, width:] = dot(hot, jnp.broadcast_to(gate, (rows, LANES)).astype(bf16), 0, 0).astype(bf16)
    copies[1].wait()
    out_ref[:, :width] = dot(hot, hidden_ref[...], 0, 0).astype(bf16)


def place_direct_kernel(members, *refs):
    out_ref = refs[-1]
    me = lax.axis_index("ex")
    tok = refs[0].shape[0]
    for s in range(members):
        out_ref[pl.ds(pl.multiple_of((me ^ s) * tok, tok), tok), :] = refs[s][...]


def place_relay_kernel(own, near, far, far_near, end, end_near, *refs):
    out_ref = refs[-1]
    me = lax.axis_index("ex")
    tok = own.shape[0]
    orders = (
        (own, near, end, end_near),
        (near, own, far, far_near),
        (far_near, far, own, near),
        (end_near, end, near, own),
    )
    for z, order in enumerate(orders):

        @pl.when(me == z)
        def _():
            for i, ref in enumerate(order):
                out_ref[i * tok : (i + 1) * tok, :] = ref[...]


def pick_kernel(dims, own_ref, other_ref, pick_ref):
    tok, top, rows, slots, groups, members, cap = dims
    tokens = members * tok
    ep, z = lax.axis_index("ep"), lax.axis_index("ex")
    chip, core = lax.shift_right_logical(ep, 1), ep & 1
    row, q = iota((rows, rows), 0), iota((rows, rows), 1)
    p = row & (cap - 1)
    step = lax.shift_right_logical(row, log2(2 * members * cap))
    wanted = (z * groups + (step ^ chip) * 2 + core) * cap + p
    choose = (wanted == q).astype(f32).astype(bf16)
    for b, ref in enumerate((own_ref, other_ref)):
        found = dot(choose, ref[...], 1, 1)
        r = iota((rows, tokens), 0)
        from_core = lax.shift_right_logical(r, log2(members * cap)) & 1
        from_z = lax.shift_right_logical(r, log2(cap)) & (members - 1)
        t = lax.shift_right_logical(iota((rows, tokens), 1), log2(tok))
        keep = (from_core == (core ^ b)) & (from_z == t)
        pick_ref[:, b * tokens : (b + 1) * tokens] = jnp.where(keep, found, 0.0).astype(bf16)


def rows_kernel(start, width, steps, pick_ref, own_ref, other_ref, *out_refs):
    out_refs = out_refs[-steps:]
    tokens = own_ref.shape[0]
    block = out_refs[0].shape[0]
    pick = pick_ref[...]
    for j in range(width // TILE):
        cols = slice(j * TILE, (j + 1) * TILE)
        took = slice(start + j * TILE, start + (j + 1) * TILE)
        got = dot(pick[:, :tokens], own_ref[:, took], 1, 0) + dot(pick[:, tokens:], other_ref[:, took], 1, 0)
        for s, ref in enumerate(out_refs):
            ref[:, cols] = got[s * block : (s + 1) * block].astype(bf16)


def order_by_step(ref, steps, block, cols):
    chip = lax.shift_right_logical(lax.axis_index("ep"), 1)
    return jnp.concatenate(
        [ref[pl.ds(pl.multiple_of((chip ^ s) * block, block), block), cols] for s in range(steps)], axis=0
    )


def low_kernel(steps, block, arrived_ref, down_ref, low_ref, gated_ref):
    hidden = down_ref.shape[1]
    rows = order_by_step(arrived_ref, steps, block, slice(0, hidden))
    gate = order_by_step(arrived_ref, steps, block, slice(hidden, hidden + LANES))[:, :1].astype(f32)
    low = dot(rows, down_ref[...], 1, 1).astype(bf16)
    low_ref[...] = low
    gated_ref[...] = (adapter_scale * gate * low.astype(f32)).astype(bf16)


def up_grad_kernel(steps, *refs):
    blocks, gated_ref, out_ref = refs[:steps], refs[steps], refs[-1]
    for j in range(out_ref.shape[1] // TILE):
        cols = slice(j * TILE, (j + 1) * TILE)
        rows = jnp.concatenate([b[:, cols] for b in blocks], axis=0)
        out_ref[:, cols] = dot(gated_ref[...], rows, 0, 0).astype(bf16)


def expert_kernel(steps, off, unread, first, final, *refs):
    blocks = refs[:steps]
    width = blocks[0].shape[1]
    tiles = width // TILE
    refs = refs[steps:]
    frozen_hbm, scale_hbm, up_hbm = refs[:3]
    refs = refs[3 + unread :]
    frozen_ref, scale_ref, up_ref, sems = refs[-4:]
    refs = refs[:-4]
    copies = fetch(
        [(scale_hbm.at[:, pl.ds(off, width)], scale_ref)]
        + [(frozen_hbm.at[:, pl.ds(off + j * TILE, TILE)], frozen_ref.at[j]) for j in range(tiles)]
        + [(up_hbm.at[:, pl.ds(off, width)], up_ref)],
        sems,
    )
    if not first:
        back_in, low_in = refs[:2]
        refs = refs[2:]
    if final:
        gated_ref, arrived_ref, down_ref, low_ref = refs[:4]
        up_grad_ref, ret_ref, back_ref, thin_ref = refs[4:]
        for j in range(tiles):
            cols = slice(j * TILE, (j + 1) * TILE)
            rows = jnp.concatenate([b[:, cols] for b in blocks], axis=0)
            up_grad_ref[:, cols] = dot(gated_ref[...], rows, 0, 0).astype(bf16)
    else:
        back_ref, thin_ref = refs
    copies[0].wait()
    for j in range(tiles):
        cols = slice(j * TILE, (j + 1) * TILE)
        rows = jnp.concatenate([b[:, cols] for b in blocks], axis=0)
        scaled = (rows.astype(f32) * scale_ref[:, cols]).astype(bf16)
        copies[1 + j].wait()
        part = dot(scaled, frozen_ref[j], 1, 1)
        if j > 0:
            part += back_ref[...]
        elif not first:
            part += back_in[...]
        back_ref[...] = part
    copies[1 + tiles].wait()
    thin = dot(jnp.concatenate([b[...] for b in blocks], axis=0), up_ref[...], 1, 1)
    thin_ref[...] = thin if first else thin + low_in[...]
    if final:
        block = blocks[0].shape[0]
        hidden = down_ref.shape[1]
        chip = lax.shift_right_logical(lax.axis_index("ep"), 1)
        saved = order_by_step(arrived_ref, steps, block, slice(0, hidden))
        gate = order_by_step(arrived_ref, steps, block, slice(hidden, hidden + LANES))[:, :1].astype(f32)
        back = back_ref[...]
        thin = thin_ref[...]
        back_low = (gate * thin).astype(bf16)
        grad = (gate * back + adapter_scale * dot(back_low, down_ref[...], 1, 0)).astype(bf16)
        gate_grad = jnp.sum(saved.astype(f32) * back, axis=1, keepdims=True) + adapter_scale * jnp.sum(
            low_ref[...].astype(f32) * thin, axis=1, keepdims=True
        )
        gate_grad = jnp.broadcast_to(gate_grad, (gate_grad.shape[0], LANES)).astype(bf16)
        for s in range(steps):
            at = pl.ds(pl.multiple_of((chip ^ s) * block, block), block)
            ret_ref[at, :hidden] = grad[s * block : (s + 1) * block]
            ret_ref[at, hidden:] = gate_grad[s * block : (s + 1) * block]
        up_grad_ref[:, width:] = (adapter_scale * dot(back_low, saved, 0, 0)).astype(bf16)


def adam_math(weights, moment, second_moment, gradient):
    weights_wide = weights.astype(f32)
    first = beta_one * moment.astype(f32) + (1.0 - beta_one) * gradient
    second = beta_two * second_moment.astype(f32) + (1.0 - beta_two) * gradient * gradient
    first_hat = first * (1.0 / (1.0 - beta_one**adam_step))
    second_hat = second * (1.0 / (1.0 - beta_two**adam_step))
    fresh = weights_wide - learn_rate * (
        first_hat / (jnp.sqrt(second_hat) + adam_eps) + weight_decay * weights_wide
    )
    return (fresh.astype(bf16), first.astype(bf16), second.astype(bf16))


def pair(partner_ref, members):
    z = lax.axis_index("ex")
    return z, partner_ref[lax.axis_index("ep") * members + z] & (members - 1)


def onward_kernel(members, hop, partner_ref, own_ref, got_ref, *refs):
    out_ref = refs[-1]
    z, mate = pair(partner_ref, members)
    if hop == 2:
        mine = ((z == 1) & (mate >= 2)) | ((z == 2) & (mate <= 1))
    else:
        mine = ((z == 1) & (mate == 0)) | ((z == 2) & (mate == 3))

    @pl.when(mine)
    def _():
        out_ref[...] = own_ref[...]

    @pl.when(jnp.logical_not(mine))
    def _():
        out_ref[...] = got_ref[...]


def adam_kernel(members, parts, unread, partner_ref, own_ref, h1, h2, h3, *refs):
    count = len(parts)
    state, refs = refs[: 3 * count], refs[3 * count + unread :]
    fresh, refs = refs[: 3 * count], refs[3 * count :]
    held, made, in_sems, out_sems = refs
    loads = []
    for n, (at, width, base) in enumerate(parts):
        for k in range(3):
            src = state[3 * n + k].at[:, pl.ds(base, width)]
            loads.append((src, held.at[k, :, pl.ds(at, width)]))
    loads = fetch(loads, in_sems)
    z, mate = pair(partner_ref, members)
    use = (
        ((z == 1) & (mate == 0)) | ((z == 2) & (mate == 3)),
        ((z == 1) & (mate >= 2)) | ((z == 2) & (mate <= 1)),
        ((z == 0) & (mate != 0)) | ((z == 3) & (mate != 3)),
    )
    stores = []
    for n, (at, width, base) in enumerate(parts):
        for load in loads[3 * n : 3 * n + 3]:
            load.wait()
        for j in range(width // TILE):
            cols = slice(at + j * TILE, at + (j + 1) * TILE)
            gradient = own_ref[:, cols].astype(f32)
            for wanted, ref in zip(use, (h1, h2, h3)):
                gradient += jnp.where(wanted, ref[:, cols].astype(f32), 0.0)
            new = adam_math(held[0, :, cols], held[1, :, cols], held[2, :, cols], gradient)
            for k in range(3):
                made[k, :, cols] = new[k]
        for k in range(3):
            dst = fresh[3 * n + k].at[:, pl.ds(base, width)]
            store = pltpu.make_async_copy(made.at[k, :, pl.ds(at, width)], dst, out_sems.at[3 * n + k])
            store.start()
            stores.append(store)
    for store in stores:
        store.wait()


def return_kernel(dims, hot_ref, ret_ref, grad_ref, gate_ref):
    tok, top, rows = dims[:3]
    hidden = grad_ref.shape[1]
    hot = hot_ref[...]
    grad_ref[...] = dot(hot, ret_ref[:, :hidden], 1, 0).astype(bf16)
    gate = dot(hot, ret_ref[:, hidden:], 1, 0)[:, :1]
    spread = jnp.where(lax.shift_right_logical(iota((rows, tok), 0), log2(top)) == iota((rows, tok), 1), gate, 0.0)
    turn = ((iota((top, rows), 1) & (top - 1)) == iota((top, rows), 0)).astype(bf16)
    gate_ref[...] = dot(turn, spread.astype(bf16), 1, 0).astype(bf16)


def shape(dims, dtype=bf16):
    return jax.ShapeDtypeStruct(dims, dtype)


def per_device(
    dout,
    gates,
    saved_down_input,
    routing,
    placement,
    partner,
    frozen,
    colscale,
    adapter_down_factor,
    adapter_up_factor,
    first_moment_down,
    second_moment_down,
    first_moment_up,
    second_moment_up,
):
    groups = lax.axis_size("ep")
    members = lax.axis_size("ex")
    slots = groups * members
    tok, top = routing.shape
    model_width = dout.shape[1]
    hidden = saved_down_input.shape[2]
    rank = adapter_down_factor.shape[2]
    rows = tok * top
    cap = rows // slots
    steps = groups // 2
    block = 2 * members * cap
    dims = (tok, top, rows, slots, groups, members, cap)
    widths = chunk_widths(model_width)
    tokens = members * tok
    assert members == 4 and groups % 2 == 0

    width0 = widths[0][1]
    rest_width = model_width - width0
    hot, chunk0, rest = call(
        functools.partial(index_kernel, dims, width0),
        [shape((rows, rows)), shape((tok, width0 + rows)), shape((tok, rest_width))],
        flops=2 * rows * rows * tok,
        moved=4 * tok * model_width,
        in_specs=[HBM] * 3,
        out_specs=[VMEM] * 3,
        scratch_shapes=[pltpu.VMEM((top, tok), jnp.int32), pltpu.VMEM((1, slots), jnp.int32), DMA((4,))],
    )(routing.T, placement.reshape(1, slots), dout)

    def other_core(x):
        return lax.ppermute(x, "ep", [(i, i ^ 1) for i in range(groups)])

    def send(x, pairs):
        return lax.ppermute(x, "ex", pairs)

    got = [send(chunk0, [(i, i ^ s) for i in range(members)]) for s in range(1, members)]

    rest = tied(rest, *got)
    middle, outer = [(1, 2), (2, 1)], [(1, 0), (2, 3)]
    near = send(rest, [(0, 1), (1, 0), (2, 3), (3, 2)])
    far = send(rest, middle)
    far_near = send(near, middle)
    end = send(far, outer)
    end_near = send(far_near, outer)

    own0 = call(
        functools.partial(place_direct_kernel, members),
        shape((tokens, width0 + rows)),
        moved=4 * tokens * width0,
    )(chunk0, *got)
    other0 = other_core(own0)
    pick = call(
        functools.partial(pick_kernel, dims),
        shape((rows, rows)),
        flops=2 * rows * rows * 2 * tokens,
        moved=4 * rows * rows,
        grid=(1,),
        in_specs=[pl.BlockSpec((tokens, rows), lambda i: (0, width0 // rows))] * 2,
        out_specs=pl.BlockSpec((rows, rows), lambda i: (0, 0)),
    )(own0, other0)
    down_t = adapter_down_factor[0].T

    def onward(hop, x, got, *after):
        moved = call(
            functools.partial(onward_kernel, members, hop),
            shape(x.shape),
            moved=4 * x.size,
            in_specs=[SMEM, VMEM, VMEM] + [ANY] * len(after),
            out_specs=VMEM,
        )(partner, x, got, *after)
        return moved, send(moved, middle if hop == 2 else outer)

    def first_hop(x):
        return send(x, [(0, 1), (3, 2)])

    def plane_rows(c, own, other, start, *after):
        off, width = widths[c]
        blocks = call(
            functools.partial(rows_kernel, start, width, steps),
            [shape((block, width))] * steps,
            flops=2 * rows * rows * width,
            moved=4 * rows * width,
            in_specs=[VMEM] * 3 + [ANY] * len(after),
            out_specs=[VMEM] * steps,
        )(pick, own, other, *after)
        sent = [lax.ppermute(blocks[s], "ep", [(i, i ^ (2 * s)) for i in range(groups)]) for s in range(1, steps)]
        return [blocks[0]] + sent

    def up_grad(blocks, *after):
        out = shape((rank, blocks[0].shape[1]))
        return call(
            functools.partial(up_grad_kernel, steps),
            out,
            flops=2 * rows * rank * out.shape[1],
            in_specs=[VMEM] * (steps + 1) + [ANY] * len(after),
            out_specs=VMEM,
        )(*blocks, gated, *after)

    def expert(c, blocks, after, *carry):
        off, width = widths[c]
        tiles = width // TILE
        final = c == len(widths) - 1
        args = list(blocks) + [frozen[0], colscale, adapter_up_factor[0]] + list(after) + list(carry)
        specs = [VMEM] * steps + [HBM] * 3 + [ANY] * len(after) + [VMEM] * len(carry)
        scratch = []
        if final:
            args += [gated, arrived, down_t, low]
            specs += [VMEM] * 4
            outs = [shape((rank, width + hidden)), shape((rows, hidden + LANES))]
            scratch = [pltpu.VMEM((rows, hidden), f32), pltpu.VMEM((rows, rank), f32)]
        else:
            outs = [shape((rows, hidden), f32), shape((rows, rank), f32)]
        scratch += [
            pltpu.VMEM((tiles, hidden, TILE), bf16),
            pltpu.VMEM((1, width), f32),
            pltpu.VMEM((rank, width), bf16),
            DMA((tiles + 2,)),
        ]
        return call(
            functools.partial(expert_kernel, steps, off, len(after), not carry, final),
            outs,
            flops=2 * rows * hidden * width,
            moved=2 * hidden * width + 2 * rows * width,
            limit=EXPERT_VMEM_LIMIT,
            in_specs=specs,
            out_specs=[VMEM] * len(outs),
            scratch_shapes=scratch,
        )(*args)

    def adam(grad, hops, parts, states, before, *after):
        total = sum(width for _, width, _ in parts)
        arrays = [x for state in states for x in state]
        carried = len(before)
        return call(
            functools.partial(adam_kernel, members, parts, carried + len(after)),
            [shape(x.shape) for x in arrays],
            flops=20 * rank * total,
            moved=20 * rank * total,
            limit=EXPERT_VMEM_LIMIT,
            in_specs=[SMEM] + [VMEM] * 4 + [HBM] * (len(arrays) + carried) + [ANY] * len(after),
            out_specs=[HBM] * len(arrays),
            input_output_aliases={5 + len(arrays) + i: i for i in range(carried)},
            scratch_shapes=[pltpu.VMEM((3, rank, total), bf16)] * 2 + [DMA((len(arrays),))] * 2,
        )(partner, grad, *hops, *arrays, *before, *after)

    up_state = [adapter_up_factor[0], first_moment_up[0], second_moment_up[0]]
    down_state = [down_t, first_moment_down[0].T, second_moment_down[0].T]
    (_, _), (off1, width1), (off2, width2) = widths

    blocks0 = plane_rows(0, own0, other0, 0)
    outgoing = call(
        functools.partial(hidden_kernel, dims),
        shape((rows, hidden + LANES)),
        flops=2 * rows * rows * hidden,
        moved=4 * rows * hidden,
        in_specs=[VMEM, HBM, HBM, ANY],
        out_specs=VMEM,
        scratch_shapes=[pltpu.VMEM((top, tok), bf16), pltpu.VMEM((rows, hidden), bf16), DMA((2,))],
    )(hot, gates.T, saved_down_input.reshape(rows, hidden), blocks0[0])

    arrived = lax.all_to_all(
        outgoing.reshape(slots, cap, hidden + LANES), ("ep", "ex"), split_axis=0, concat_axis=0, tiled=True
    ).reshape(rows, hidden + LANES)

    low, gated = call(
        functools.partial(low_kernel, steps, block),
        [shape((rows, rank)), shape((rows, rank))],
        flops=2 * rows * hidden * rank,
        moved=2 * rows * hidden,
    )(arrived, down_t)

    own1 = call(
        place_relay_kernel,
        shape((tokens, rest_width)),
        moved=4 * tokens * rest_width,
        in_specs=[VMEM] * 6 + [ANY] * steps,
        out_specs=VMEM,
    )(rest, near, far, far_near, end, end_near, outgoing, *blocks0[1:])
    other1 = other_core(own1)
    blocks1 = plane_rows(1, own1, other1, 0)
    blocks2 = plane_rows(2, own1, other1, width1, blocks1[0])
    grad0 = up_grad(blocks0, blocks2[0])
    carry0 = expert(0, blocks0, [grad0])
    grad1 = up_grad(blocks1, carry0[0])
    first0 = first_hop(grad0)
    first1 = first_hop(grad1)
    msecond0, second0 = onward(2, grad0, first0, grad1)
    carry1 = expert(1, blocks1, [grad1], *carry0)
    mthird0, third0 = onward(3, grad0, second0, carry1[0])
    msecond1, second1 = onward(2, grad1, first1, carry1[0])
    grad2, ret = expert(2, blocks2, [carry1[0], mthird0, first1], *carry1)
    first2 = first_hop(grad2)
    returned = lax.all_to_all(
        ret.reshape(slots, cap, hidden + LANES), ("ep", "ex"), split_axis=0, concat_axis=0, tiled=True
    ).reshape(rows, hidden + LANES)
    mthird1, third1 = onward(3, grad1, second1, ret)
    fresh_up = adam(grad0, (first0, second0, third0), [(0, width0, 0)], [up_state], [], ret)
    msecond2, second2 = onward(2, grad2, first2, ret)
    row_grad, gate_grad = call(
        functools.partial(return_kernel, dims),
        [shape((rows, hidden)), shape((top, tok))],
        flops=2 * rows * rows * hidden,
        moved=4 * rows * hidden,
    )(hot, returned)
    mthird2, third2 = onward(3, grad2, second2, fresh_up[0])
    fresh_up = adam(grad1, (first1, second1, third1), [(0, width1, off1)], [up_state], fresh_up)
    fresh = adam(
        grad2,
        (first2, second2, third2),
        [(0, width2, off2), (width2, hidden, 0)],
        [up_state, down_state],
        fresh_up,
    )
    fresh_up, fresh_down = fresh[:3], fresh[3:]

    return (
        row_grad.reshape(tok, top, hidden),
        gate_grad.T,
        fresh_down[0].T[None],
        fresh_up[0][None],
        fresh_down[1].T[None],
        fresh_down[2].T[None],
        fresh_up[1][None],
        fresh_up[2][None],
    )


def solution(mesh):
    two = P(("ep", "ex"), None)
    three = P(("ep", "ex"), None, None)
    return jax.shard_map(
        per_device,
        mesh=mesh,
        in_specs=(two, two, three, two, P(), P(), three, two) + (three,) * 6,
        out_specs=(three, two) + (three,) * 6,
        check_vma=False,
    )
```

```python
import functools

import jax
import jax.numpy as jnp
from jax import lax
from jax.experimental import pallas as pl
from jax.experimental.pallas import tpu as pltpu
from jax.sharding import PartitionSpec as P

adapter_scale = 2.0
beta_one = 0.9
beta_two = 0.999
adam_eps = 1e-08
learn_rate = 0.01
weight_decay = 0.01
adam_step = 10

TILE = 512
LANES = 128
SHARES = (5, 6, 3)
VMEM_LIMIT = 24 * 1024 * 1024
EXPERT_VMEM_LIMIT = 42 * 1024 * 1024
bf16 = jnp.bfloat16
f32 = jnp.float32


def chunk_widths(width):
    tiles = width // TILE
    total = sum(SHARES)
    edges = [0]
    taken = 0
    for share in SHARES:
        taken += share
        edges.append(tiles * taken // total)
    return [(edges[i] * TILE, (edges[i + 1] - edges[i]) * TILE) for i in range(len(SHARES)) if edges[i + 1] > edges[i]]


def log2(n):
    k = n.bit_length() - 1
    assert 1 << k == n
    return k


def iota(shape, dim):
    return lax.broadcasted_iota(jnp.int32, shape, dim)


def dot(a, b, ca, cb):
    return lax.dot_general(a, b, (((ca,), (cb,)), ((), ())), preferred_element_type=f32)


HBM = pl.BlockSpec(memory_space=pltpu.HBM)
VMEM = pl.BlockSpec(memory_space=pltpu.VMEM)
SMEM = pl.BlockSpec(memory_space=pltpu.SMEM)
ANY = pl.BlockSpec(memory_space=pl.ANY)
DMA = pltpu.SemaphoreType.DMA


def fetch(pairs, sems):
    copies = [pltpu.make_async_copy(src, dst, sems.at[i]) for i, (src, dst) in enumerate(pairs)]
    for copy in copies:
        copy.start()
    return copies


def call(kernel, outs, flops=0, moved=0, limit=VMEM_LIMIT, **kw):
    params = pltpu.CompilerParams(vmem_limit_bytes=limit)
    cost = pl.CostEstimate(flops=flops, bytes_accessed=moved, transcendentals=0)
    return pl.pallas_call(kernel, out_shape=outs, compiler_params=params, cost_estimate=cost, **kw)


def index_kernel(dims, width, rout_hbm, place_hbm, dout_hbm, hot_ref, chunk_ref, rest_ref, rout_ref, place_ref, sems):
    rest_width = rest_ref.shape[1]
    copies = fetch(
        [
            (rout_hbm, rout_ref),
            (place_hbm, place_ref),
            (dout_hbm.at[:, pl.ds(0, width)], chunk_ref.at[:, pl.ds(0, width)]),
            (dout_hbm.at[:, pl.ds(width, rest_width)], rest_ref),
        ],
        sems,
    )
    copies[0].wait()
    copies[1].wait()
    tok, top, rows, slots, groups, members, cap = dims
    kt = log2(top)
    rid_c, rid_r = iota((rows, 1), 0), iota((1, rows), 1)
    spread = (lax.shift_right_logical(iota((rows, tok), 0), kt) == iota((rows, tok), 1)).astype(bf16)
    routes = rout_ref[...].astype(f32).astype(bf16)
    wide = dot(spread, routes, 1, 1)
    e_col = jnp.sum(jnp.where((iota((rows, top), 0) & (top - 1)) == iota((rows, top), 1), wide, 0.0), axis=1, keepdims=True)
    tall = dot(routes, spread, 1, 1)
    e_row = jnp.sum(jnp.where((iota((top, rows), 1) & (top - 1)) == iota((top, rows), 0), tall, 0.0), axis=0, keepdims=True)
    earlier = rid_r < rid_c
    turn = jnp.sum(jnp.where((e_col == e_row) & earlier, 1.0, 0.0), axis=1, keepdims=True).astype(jnp.int32)
    holds = e_col == place_ref[...].astype(f32)
    slot = iota((rows, slots), 1).astype(f32)
    first = jnp.min(jnp.where(holds, slot, float(slots)), axis=1, keepdims=True)
    last = jnp.max(jnp.where(holds, slot, -1.0), axis=1, keepdims=True)
    target = jnp.where((turn & 1) == 1, last, first)
    target_row = jnp.sum(jnp.where(rid_c == rid_r, target, 0.0), axis=0, keepdims=True)
    pos = jnp.sum(jnp.where((target == target_row) & earlier, 1.0, 0.0), axis=1, keepdims=True).astype(jnp.int32)
    target = target.astype(jnp.int32)
    place = target * cap + pos
    place_z = ((target & (members - 1)) * groups + lax.shift_right_logical(target, log2(members))) * cap + pos
    hot_ref[...] = (place == rid_r).astype(f32).astype(bf16)
    hot_z = (place_z == rid_r).astype(f32).astype(bf16)
    chunk_ref[:, width:] = dot(spread, hot_z, 0, 0).astype(bf16)
    copies[2].wait()
    copies[3].wait()


def tied_kernel(*refs):
    pass


def tied(x, *after):
    return call(
        tied_kernel,
        shape(x.shape),
        in_specs=[ANY] * (1 + len(after)),
        out_specs=ANY,
        input_output_aliases={0: 0},
    )(x, *after)


def hidden_kernel(dims, hot_ref, gate_hbm, hidden_hbm, after_ref, out_ref, gate_ref, hidden_ref, sems):
    tok, top, rows = dims[:3]
    copies = fetch([(gate_hbm, gate_ref), (hidden_hbm, hidden_ref)], sems)
    copies[0].wait()
    width = hidden_ref.shape[1]
    hot = hot_ref[...]
    spread = (lax.shift_right_logical(iota((rows, tok), 0), log2(top)) == iota((rows, tok), 1)).astype(bf16)
    wide = dot(spread, gate_ref[...], 1, 1)
    gate = jnp.sum(jnp.where((iota((rows, top), 0) & (top - 1)) == iota((rows, top), 1), wide, 0.0), axis=1, keepdims=True)
    out_ref[:, width:] = dot(hot, jnp.broadcast_to(gate, (rows, LANES)).astype(bf16), 0, 0).astype(bf16)
    copies[1].wait()
    out_ref[:, :width] = dot(hot, hidden_ref[...], 0, 0).astype(bf16)


def place_direct_kernel(members, *refs):
    out_ref = refs[-1]
    me = lax.axis_index("ex")
    tok = refs[0].shape[0]
    for s in range(members):
        out_ref[pl.ds(pl.multiple_of((me ^ s) * tok, tok), tok), :] = refs[s][...]


def place_relay_kernel(own, near, far, far_near, end, end_near, *refs):
    out_ref = refs[-1]
    me = lax.axis_index("ex")
    tok = own.shape[0]
    orders = (
        (own, near, end, end_near),
        (near, own, far, far_near),
        (far_near, far, own, near),
        (end_near, end, near, own),
    )
    for z, order in enumerate(orders):

        @pl.when(me == z)
        def _():
            for i, ref in enumerate(order):
                out_ref[i * tok : (i + 1) * tok, :] = ref[...]


def pick_kernel(dims, own_ref, other_ref, pick_ref):
    tok, top, rows, slots, groups, members, cap = dims
    tokens = members * tok
    ep, z = lax.axis_index("ep"), lax.axis_index("ex")
    chip, core = lax.shift_right_logical(ep, 1), ep & 1
    row, q = iota((rows, rows), 0), iota((rows, rows), 1)
    p = row & (cap - 1)
    step = lax.shift_right_logical(row, log2(2 * members * cap))
    wanted = (z * groups + (step ^ chip) * 2 + core) * cap + p
    choose = (wanted == q).astype(f32).astype(bf16)
    for b, ref in enumerate((own_ref, other_ref)):
        found = dot(choose, ref[...], 1, 1)
        r = iota((rows, tokens), 0)
        from_core = lax.shift_right_logical(r, log2(members * cap)) & 1
        from_z = lax.shift_right_logical(r, log2(cap)) & (members - 1)
        t = lax.shift_right_logical(iota((rows, tokens), 1), log2(tok))
        keep = (from_core == (core ^ b)) & (from_z == t)
        pick_ref[:, b * tokens : (b + 1) * tokens] = jnp.where(keep, found, 0.0).astype(bf16)


def rows_kernel(start, width, steps, pick_ref, own_ref, other_ref, *out_refs):
    out_refs = out_refs[-steps:]
    tokens = own_ref.shape[0]
    block = out_refs[0].shape[0]
    pick = pick_ref[...]
    for j in range(width // TILE):
        cols = slice(j * TILE, (j + 1) * TILE)
        took = slice(start + j * TILE, start + (j + 1) * TILE)
        got = dot(pick[:, :tokens], own_ref[:, took], 1, 0) + dot(pick[:, tokens:], other_ref[:, took], 1, 0)
        for s, ref in enumerate(out_refs):
            ref[:, cols] = got[s * block : (s + 1) * block].astype(bf16)


def order_by_step(ref, steps, block, cols):
    chip = lax.shift_right_logical(lax.axis_index("ep"), 1)
    return jnp.concatenate(
        [ref[pl.ds(pl.multiple_of((chip ^ s) * block, block), block), cols] for s in range(steps)], axis=0
    )


def low_kernel(steps, block, arrived_ref, down_ref, low_ref, gated_ref):
    hidden = down_ref.shape[1]
    rows = order_by_step(arrived_ref, steps, block, slice(0, hidden))
    gate = order_by_step(arrived_ref, steps, block, slice(hidden, hidden + LANES))[:, :1].astype(f32)
    low = dot(rows, down_ref[...], 1, 1).astype(bf16)
    low_ref[...] = low
    gated_ref[...] = (adapter_scale * gate * low.astype(f32)).astype(bf16)


def up_grad_kernel(steps, *refs):
    blocks, gated_ref, out_ref = refs[:steps], refs[steps], refs[-1]
    for j in range(out_ref.shape[1] // TILE):
        cols = slice(j * TILE, (j + 1) * TILE)
        rows = jnp.concatenate([b[:, cols] for b in blocks], axis=0)
        out_ref[:, cols] = dot(gated_ref[...], rows, 0, 0).astype(bf16)


def expert_kernel(steps, off, unread, first, final, *refs):
    blocks = refs[:steps]
    width = blocks[0].shape[1]
    tiles = width // TILE
    refs = refs[steps:]
    frozen_hbm, scale_hbm, up_hbm = refs[:3]
    refs = refs[3 + unread :]
    frozen_ref, scale_ref, up_ref, sems = refs[-4:]
    refs = refs[:-4]
    copies = fetch(
        [(scale_hbm.at[:, pl.ds(off, width)], scale_ref)]
        + [(frozen_hbm.at[:, pl.ds(off + j * TILE, TILE)], frozen_ref.at[j]) for j in range(tiles)]
        + [(up_hbm.at[:, pl.ds(off, width)], up_ref)],
        sems,
    )
    if not first:
        back_in, low_in = refs[:2]
        refs = refs[2:]
    if final:
        gated_ref, arrived_ref, down_ref, low_ref = refs[:4]
        up_grad_ref, ret_ref, back_ref, thin_ref = refs[4:]
        for j in range(tiles):
            cols = slice(j * TILE, (j + 1) * TILE)
            rows = jnp.concatenate([b[:, cols] for b in blocks], axis=0)
            up_grad_ref[:, cols] = dot(gated_ref[...], rows, 0, 0).astype(bf16)
    else:
        back_ref, thin_ref = refs
    copies[0].wait()
    for j in range(tiles):
        cols = slice(j * TILE, (j + 1) * TILE)
        rows = jnp.concatenate([b[:, cols] for b in blocks], axis=0)
        scaled = (rows.astype(f32) * scale_ref[:, cols]).astype(bf16)
        copies[1 + j].wait()
        part = dot(scaled, frozen_ref[j], 1, 1)
        if j > 0:
            part += back_ref[...]
        elif not first:
            part += back_in[...]
        back_ref[...] = part
    copies[1 + tiles].wait()
    thin = dot(jnp.concatenate([b[...] for b in blocks], axis=0), up_ref[...], 1, 1)
    thin_ref[...] = thin if first else thin + low_in[...]
    if final:
        block = blocks[0].shape[0]
        hidden = down_ref.shape[1]
        chip = lax.shift_right_logical(lax.axis_index("ep"), 1)
        saved = order_by_step(arrived_ref, steps, block, slice(0, hidden))
        gate = order_by_step(arrived_ref, steps, block, slice(hidden, hidden + LANES))[:, :1].astype(f32)
        back = back_ref[...]
        thin = thin_ref[...]
        back_low = (gate * thin).astype(bf16)
        grad = (gate * back + adapter_scale * dot(back_low, down_ref[...], 1, 0)).astype(bf16)
        gate_grad = jnp.sum(saved.astype(f32) * back, axis=1, keepdims=True) + adapter_scale * jnp.sum(
            low_ref[...].astype(f32) * thin, axis=1, keepdims=True
        )
        gate_grad = jnp.broadcast_to(gate_grad, (gate_grad.shape[0], LANES)).astype(bf16)
        for s in range(steps):
            at = pl.ds(pl.multiple_of((chip ^ s) * block, block), block)
            ret_ref[at, :hidden] = grad[s * block : (s + 1) * block]
            ret_ref[at, hidden:] = gate_grad[s * block : (s + 1) * block]
        up_grad_ref[:, width:] = (adapter_scale * dot(back_low, saved, 0, 0)).astype(bf16)


def adam_math(weights, moment, second_moment, gradient):
    weights_wide = weights.astype(f32)
    first = beta_one * moment.astype(f32) + (1.0 - beta_one) * gradient
    second = beta_two * second_moment.astype(f32) + (1.0 - beta_two) * gradient * gradient
    first_hat = first * (1.0 / (1.0 - beta_one**adam_step))
    second_hat = second * (1.0 / (1.0 - beta_two**adam_step))
    fresh = weights_wide - learn_rate * (
        first_hat / (jnp.sqrt(second_hat) + adam_eps) + weight_decay * weights_wide
    )
    return (fresh.astype(bf16), first.astype(bf16), second.astype(bf16))


def pair(partner_ref, members):
    z = lax.axis_index("ex")
    return z, partner_ref[lax.axis_index("ep") * members + z] & (members - 1)


def onward_kernel(members, hop, partner_ref, own_ref, got_ref, *refs):
    out_ref = refs[-1]
    z, mate = pair(partner_ref, members)
    if hop == 2:
        mine = ((z == 1) & (mate >= 2)) | ((z == 2) & (mate <= 1))
    else:
        mine = ((z == 1) & (mate == 0)) | ((z == 2) & (mate == 3))

    @pl.when(mine)
    def _():
        out_ref[...] = own_ref[...]

    @pl.when(jnp.logical_not(mine))
    def _():
        out_ref[...] = got_ref[...]


def adam_kernel(members, parts, unread, partner_ref, own_ref, h1, h2, h3, *refs):
    count = len(parts)
    state, refs = refs[: 3 * count], refs[3 * count + unread :]
    fresh, refs = refs[: 3 * count], refs[3 * count :]
    held, made, in_sems, out_sems = refs
    loads = []
    for n, (at, width, base) in enumerate(parts):
        for k in range(3):
            src = state[3 * n + k].at[:, pl.ds(base, width)]
            loads.append((src, held.at[k, :, pl.ds(at, width)]))
    loads = fetch(loads, in_sems)
    z, mate = pair(partner_ref, members)
    use = (
        ((z == 1) & (mate == 0)) | ((z == 2) & (mate == 3)),
        ((z == 1) & (mate >= 2)) | ((z == 2) & (mate <= 1)),
        ((z == 0) & (mate != 0)) | ((z == 3) & (mate != 3)),
    )
    stores = []
    for n, (at, width, base) in enumerate(parts):
        for load in loads[3 * n : 3 * n + 3]:
            load.wait()
        for j in range(width // TILE):
            cols = slice(at + j * TILE, at + (j + 1) * TILE)
            gradient = own_ref[:, cols].astype(f32)
            for wanted, ref in zip(use, (h1, h2, h3)):
                gradient += jnp.where(wanted, ref[:, cols].astype(f32), 0.0)
            new = adam_math(held[0, :, cols], held[1, :, cols], held[2, :, cols], gradient)
            for k in range(3):
                made[k, :, cols] = new[k]
        for k in range(3):
            dst = fresh[3 * n + k].at[:, pl.ds(base, width)]
            store = pltpu.make_async_copy(made.at[k, :, pl.ds(at, width)], dst, out_sems.at[3 * n + k])
            store.start()
            stores.append(store)
    for store in stores:
        store.wait()


def return_kernel(dims, hot_ref, ret_ref, grad_ref, gate_ref):
    tok, top, rows = dims[:3]
    hidden = grad_ref.shape[1]
    hot = hot_ref[...]
    grad_ref[...] = dot(hot, ret_ref[:, :hidden], 1, 0).astype(bf16)
    gate = dot(hot, ret_ref[:, hidden:], 1, 0)[:, :1]
    spread = jnp.where(lax.shift_right_logical(iota((rows, tok), 0), log2(top)) == iota((rows, tok), 1), gate, 0.0)
    turn = ((iota((top, rows), 1) & (top - 1)) == iota((top, rows), 0)).astype(bf16)
    gate_ref[...] = dot(turn, spread.astype(bf16), 1, 0).astype(bf16)


def shape(dims, dtype=bf16):
    return jax.ShapeDtypeStruct(dims, dtype)


def per_device(
    dout,
    gates,
    saved_down_input,
    routing,
    placement,
    partner,
    frozen,
    colscale,
    adapter_down_factor,
    adapter_up_factor,
    first_moment_down,
    second_moment_down,
    first_moment_up,
    second_moment_up,
):
    groups = lax.axis_size("ep")
    members = lax.axis_size("ex")
    slots = groups * members
    tok, top = routing.shape
    model_width = dout.shape[1]
    hidden = saved_down_input.shape[2]
    rank = adapter_down_factor.shape[2]
    rows = tok * top
    cap = rows // slots
    steps = groups // 2
    block = 2 * members * cap
    dims = (tok, top, rows, slots, groups, members, cap)
    widths = chunk_widths(model_width)
    tokens = members * tok
    assert members == 4 and groups % 2 == 0

    width0 = widths[0][1]
    rest_width = model_width - width0
    hot, chunk0, rest = call(
        functools.partial(index_kernel, dims, width0),
        [shape((rows, rows)), shape((tok, width0 + rows)), shape((tok, rest_width))],
        flops=2 * rows * rows * tok,
        moved=4 * tok * model_width,
        in_specs=[HBM] * 3,
        out_specs=[VMEM] * 3,
        scratch_shapes=[pltpu.VMEM((top, tok), jnp.int32), pltpu.VMEM((1, slots), jnp.int32), DMA((4,))],
    )(routing.T, placement.reshape(1, slots), dout)

    def other_core(x):
        return lax.ppermute(x, "ep", [(i, i ^ 1) for i in range(groups)])

    def send(x, pairs):
        return lax.ppermute(x, "ex", pairs)

    got = [send(chunk0, [(i, i ^ s) for i in range(members)]) for s in range(1, members)]

    rest = tied(rest, got[0])
    middle, outer = [(1, 2), (2, 1)], [(1, 0), (2, 3)]
    near = send(rest, [(0, 1), (1, 0), (2, 3), (3, 2)])
    far = send(rest, middle)
    far_near = send(near, middle)
    end = send(far, outer)
    end_near = send(far_near, outer)

    own0 = call(
        functools.partial(place_direct_kernel, members),
        shape((tokens, width0 + rows)),
        moved=4 * tokens * width0,
    )(chunk0, *got)
    other0 = other_core(own0)
    pick = call(
        functools.partial(pick_kernel, dims),
        shape((rows, rows)),
        flops=2 * rows * rows * 2 * tokens,
        moved=4 * rows * rows,
        grid=(1,),
        in_specs=[pl.BlockSpec((tokens, rows), lambda i: (0, width0 // rows))] * 2,
        out_specs=pl.BlockSpec((rows, rows), lambda i: (0, 0)),
    )(own0, other0)
    down_t = adapter_down_factor[0].T

    def onward(hop, x, got, *after):
        moved = call(
            functools.partial(onward_kernel, members, hop),
            shape(x.shape),
            moved=4 * x.size,
            in_specs=[SMEM, VMEM, VMEM] + [ANY] * len(after),
            out_specs=VMEM,
        )(partner, x, got, *after)
        return moved, send(moved, middle if hop == 2 else outer)

    def first_hop(x):
        return send(x, [(0, 1), (3, 2)])

    def plane_rows(c, own, other, start, *after):
        off, width = widths[c]
        blocks = call(
            functools.partial(rows_kernel, start, width, steps),
            [shape((block, width))] * steps,
            flops=2 * rows * rows * width,
            moved=4 * rows * width,
            in_specs=[VMEM] * 3 + [ANY] * len(after),
            out_specs=[VMEM] * steps,
        )(pick, own, other, *after)
        sent = [lax.ppermute(blocks[s], "ep", [(i, i ^ (2 * s)) for i in range(groups)]) for s in range(1, steps)]
        return [blocks[0]] + sent

    def up_grad(blocks, *after):
        out = shape((rank, blocks[0].shape[1]))
        return call(
            functools.partial(up_grad_kernel, steps),
            out,
            flops=2 * rows * rank * out.shape[1],
            in_specs=[VMEM] * (steps + 1) + [ANY] * len(after),
            out_specs=VMEM,
        )(*blocks, gated, *after)

    def expert(c, blocks, after, *carry):
        off, width = widths[c]
        tiles = width // TILE
        final = c == len(widths) - 1
        args = list(blocks) + [frozen[0], colscale, adapter_up_factor[0]] + list(after) + list(carry)
        specs = [VMEM] * steps + [HBM] * 3 + [ANY] * len(after) + [VMEM] * len(carry)
        scratch = []
        if final:
            args += [gated, arrived, down_t, low]
            specs += [VMEM] * 4
            outs = [shape((rank, width + hidden)), shape((rows, hidden + LANES))]
            scratch = [pltpu.VMEM((rows, hidden), f32), pltpu.VMEM((rows, rank), f32)]
        else:
            outs = [shape((rows, hidden), f32), shape((rows, rank), f32)]
        scratch += [
            pltpu.VMEM((tiles, hidden, TILE), bf16),
            pltpu.VMEM((1, width), f32),
            pltpu.VMEM((rank, width), bf16),
            DMA((tiles + 2,)),
        ]
        return call(
            functools.partial(expert_kernel, steps, off, len(after), not carry, final),
            outs,
            flops=2 * rows * hidden * width,
            moved=2 * hidden * width + 2 * rows * width,
            limit=EXPERT_VMEM_LIMIT,
            in_specs=specs,
            out_specs=[VMEM] * len(outs),
            scratch_shapes=scratch,
        )(*args)

    def adam(grad, hops, parts, states, before, *after):
        total = sum(width for _, width, _ in parts)
        arrays = [x for state in states for x in state]
        carried = len(before)
        return call(
            functools.partial(adam_kernel, members, parts, carried + len(after)),
            [shape(x.shape) for x in arrays],
            flops=20 * rank * total,
            moved=20 * rank * total,
            limit=EXPERT_VMEM_LIMIT,
            in_specs=[SMEM] + [VMEM] * 4 + [HBM] * (len(arrays) + carried) + [ANY] * len(after),
            out_specs=[HBM] * len(arrays),
            input_output_aliases={5 + len(arrays) + i: i for i in range(carried)},
            scratch_shapes=[pltpu.VMEM((3, rank, total), bf16)] * 2 + [DMA((len(arrays),))] * 2,
        )(partner, grad, *hops, *arrays, *before, *after)

    up_state = [adapter_up_factor[0], first_moment_up[0], second_moment_up[0]]
    down_state = [down_t, first_moment_down[0].T, second_moment_down[0].T]
    (_, _), (off1, width1), (off2, width2) = widths

    blocks0 = plane_rows(0, own0, other0, 0)
    outgoing = call(
        functools.partial(hidden_kernel, dims),
        shape((rows, hidden + LANES)),
        flops=2 * rows * rows * hidden,
        moved=4 * rows * hidden,
        in_specs=[VMEM, HBM, HBM, ANY],
        out_specs=VMEM,
        scratch_shapes=[pltpu.VMEM((top, tok), bf16), pltpu.VMEM((rows, hidden), bf16), DMA((2,))],
    )(hot, gates.T, saved_down_input.reshape(rows, hidden), blocks0[0])

    arrived = lax.all_to_all(
        outgoing.reshape(slots, cap, hidden + LANES), ("ep", "ex"), split_axis=0, concat_axis=0, tiled=True
    ).reshape(rows, hidden + LANES)

    low, gated = call(
        functools.partial(low_kernel, steps, block),
        [shape((rows, rank)), shape((rows, rank))],
        flops=2 * rows * hidden * rank,
        moved=2 * rows * hidden,
    )(arrived, down_t)

    own1 = call(
        place_relay_kernel,
        shape((tokens, rest_width)),
        moved=4 * tokens * rest_width,
        in_specs=[VMEM] * 6 + [ANY] * steps,
        out_specs=VMEM,
    )(rest, near, far, far_near, end, end_near, outgoing, *blocks0[1:])
    other1 = other_core(own1)
    blocks1 = plane_rows(1, own1, other1, 0)
    blocks2 = plane_rows(2, own1, other1, width1, blocks1[0])
    grad0 = up_grad(blocks0, blocks2[0])
    carry0 = expert(0, blocks0, [grad0])
    grad1 = up_grad(blocks1, carry0[0])
    first0 = first_hop(grad0)
    first1 = first_hop(grad1)
    msecond0, second0 = onward(2, grad0, first0, grad1)
    carry1 = expert(1, blocks1, [grad1], *carry0)
    mthird0, third0 = onward(3, grad0, second0, carry1[0])
    msecond1, second1 = onward(2, grad1, first1, carry1[0])
    grad2, ret = expert(2, blocks2, [carry1[0], mthird0, first1], *carry1)
    first2 = first_hop(grad2)
    returned = lax.all_to_all(
        ret.reshape(slots, cap, hidden + LANES), ("ep", "ex"), split_axis=0, concat_axis=0, tiled=True
    ).reshape(rows, hidden + LANES)
    mthird1, third1 = onward(3, grad1, second1, ret)
    fresh_up = adam(grad0, (first0, second0, third0), [(0, width0, 0)], [up_state], [], ret)
    msecond2, second2 = onward(2, grad2, first2, ret)
    row_grad, gate_grad = call(
        functools.partial(return_kernel, dims),
        [shape((rows, hidden)), shape((top, tok))],
        flops=2 * rows * rows * hidden,
        moved=4 * rows * hidden,
    )(hot, returned)
    mthird2, third2 = onward(3, grad2, second2, fresh_up[0])
    fresh_up = adam(grad1, (first1, second1, third1), [(0, width1, off1)], [up_state], fresh_up)
    fresh = adam(
        grad2,
        (first2, second2, third2),
        [(0, width2, off2), (width2, hidden, 0)],
        [up_state, down_state],
        fresh_up,
    )
    fresh_up, fresh_down = fresh[:3], fresh[3:]

    return (
        row_grad.reshape(tok, top, hidden),
        gate_grad.T,
        fresh_down[0].T[None],
        fresh_up[0][None],
        fresh_down[1].T[None],
        fresh_down[2].T[None],
        fresh_up[1][None],
        fresh_up[2][None],
    )


def solution(mesh):
    two = P(("ep", "ex"), None)
    three = P(("ep", "ex"), None, None)
    return jax.shard_map(
        per_device,
        mesh=mesh,
        in_specs=(two, two, three, two, P(), P(), three, two) + (three,) * 6,
        out_specs=(three, two) + (three,) * 6,
        check_vma=False,
    )
```
